512 devices in a mesh: grp: 64 (over y, x, core), batch: 8 (over z).
Axes of the slice: x: 4, y: 8, z: 8, core: 2. Of those that a mesh axis runs over, the one named last changes fastest.
Arguments:
- tokens: bfloat16 [512, 8, 16384], P('batch', None, 'grp'), may hold values from -6 to 6
- input_weights: bfloat16 [2, 1024, 65536], P(None, 'batch', 'grp'), may hold values from -0.1875 to 0.1875
- recur_weights: bfloat16 [2, 1024, 65536], P(None, 'batch', 'grp'), may hold values from -0.1875 to 0.1875
- biases: float32 [2, 65536], P(None, 'grp'), may hold values from -1 to 4
- shuffle: int32 [16384], replicated, may hold values from 0 to 16383, as said below
Outputs:
- second_states: bfloat16 [512, 8, 16384], P('batch', None, 'grp')
The draws below stay inside these ranges and needn't reach their ends.
Inputs may be any that keep to these rules, and one draw needn't show every extreme that they name: shuffle is a permutation of the 16384 channels. Position j * 256 + s * 4 + k (k below 4) holds a channel of block s, that is one in [s * 256, (s + 1) * 256).
All inputs are finite; a program needn't handle non-finite values.
Results may differ from the reference program's by a relative error of at most 0.0034.
Values may be sent and summed in bfloat16 or wider, within the bound.
A program may use at most 64 MiB of HBM per device.

```python
import jax
import jax.numpy as jnp

UNITS = 16384
GROUPS = 16
STEPS = 8
SEQS = 512
GROUP_WIDTH = 1024
UNIT_DEV = 256
SPLIT = 4
KSLOT = 4
N_GRP = 64


def draw_biases(key, part):
    key = jax.random.fold_in(key, 11)
    first_key, second_key = jax.random.split(key)
    column = jnp.arange(4 * UNITS, dtype=jnp.int32)
    gate_kind = column // UNIT_DEV % 4
    forget_vals = jax.random.uniform(first_key, (2, 4 * UNITS), jnp.float32, 0.0, 4.0)
    other_vals = jax.random.uniform(second_key, (2, 4 * UNITS), jnp.float32, -1.0, 1.0)
    return jnp.where(gate_kind[None, :] == 1, forget_vals, other_vals)


def draw_shuffle(key, part):
    key = jax.random.fold_in(key, 23)
    keys = jax.random.split(key, N_GRP)
    orders = jax.vmap(lambda single: jax.random.permutation(single, UNIT_DEV))(keys)
    orders = orders.astype(jnp.int32).reshape(N_GRP, N_GRP, KSLOT)
    source = jnp.arange(N_GRP, dtype=jnp.int32)[:, None, None] * UNIT_DEV
    table = jnp.transpose(orders + source, (1, 0, 2))
    return table.reshape(UNITS)


def shard_levels(key, dims, cuts, smallest, largest):
    factor_of = 1.0
    for axis_at, parts in cuts:
        steps = jax.random.uniform(jax.random.fold_in(jax.random.fold_in(key, 6), axis_at), (parts,), jnp.float32, smallest / len(cuts), largest / len(cuts))
        factor_of = factor_of * jnp.repeat(jnp.exp(steps), dims[axis_at] // parts).reshape((-1,) + (1,) * (len(dims) - 1 - axis_at))
    return factor_of


def normal_values(key, shape, scale, most, cuts=(), held_as=jnp.bfloat16):
    array = jax.random.normal(key, shape, jnp.float32) * scale
    if len(cuts) > 0:
        array = shard_levels(key, shape, cuts, -0.22, 0.18) * array
    return jnp.clip(array, min=-most, max=most).astype(held_as)


def setup_inputs(seed: int = 0) -> dict:
    key_of = jax.random.split(jax.random.key(seed), 6)
    return {
        "tokens": normal_values(key_of[0], (SEQS, STEPS, UNITS), 1.0, 6.0, ((0, 8), (2, 64))),
        "input_weights": normal_values(key_of[1], (2, GROUP_WIDTH, 4 * UNITS), GROUP_WIDTH ** -0.5, 0.1875, ((1, 8), (2, 64))),
        "recur_weights": normal_values(key_of[2], (2, GROUP_WIDTH, 4 * UNITS), GROUP_WIDTH ** -0.5, 0.1875, ((1, 8), (2, 64))),
        "biases": draw_biases(jax.random.fold_in(key_of[5], 71), 0),
        "shuffle": draw_shuffle(jax.random.fold_in(key_of[5], 71), 0),
    }


def run_group(inputs, w_in, w_rec, bias):
    seqs, steps, width = inputs.shape
    proj = jnp.dot(inputs.reshape(seqs * steps, width), w_in, preferred_element_type=jnp.float32).reshape(seqs, steps, 4 * width)
    state = jnp.zeros((seqs, width), jnp.bfloat16)
    cell = jnp.zeros((seqs, width), jnp.float32)
    outputs = []
    for step in range(steps):
        pre = proj[:, step] + jnp.dot(state, w_rec, preferred_element_type=jnp.float32) + bias
        pre = pre.reshape(seqs, SPLIT, 4, UNIT_DEV)
        ingate = jax.nn.sigmoid(pre[:, :, 0]).reshape(seqs, width)
        forget = jax.nn.sigmoid(pre[:, :, 1]).reshape(seqs, width)
        cellgate = jnp.tanh(pre[:, :, 2]).reshape(seqs, width)
        outgate = jax.nn.sigmoid(pre[:, :, 3]).reshape(seqs, width)
        cell = forget * cell + ingate * cellgate
        state = (outgate * jnp.tanh(cell)).astype(jnp.bfloat16)
        outputs.append(state)
    return jnp.stack(outputs, axis=1)


def run_layer(inputs, w_in, w_rec, bias):
    pieces = []
    width = GROUP_WIDTH
    for group in range(GROUPS):
        chans = inputs[:, :, group * width:(group + 1) * width]
        cols = slice(4 * group * width, 4 * (group + 1) * width)
        pieces.append(run_group(chans, w_in[:, cols], w_rec[:, cols], bias[cols]))
    return jnp.concatenate(pieces, axis=2)


def reference(tokens, input_weights, recur_weights, biases, shuffle):
    first = run_layer(tokens, input_weights[0], recur_weights[0], biases[0])
    mixed = jnp.take(first, shuffle, axis=2)
    return run_layer(mixed, input_weights[1], recur_weights[1], biases[1])
```

```python
import jax
import jax.numpy as jnp
from jax import lax
from jax.experimental import pallas as pl
from jax.experimental.pallas import tpu as pltpu
from jax.sharding import PartitionSpec as P

MESH = pl.DeviceIdType.MESH
DEPTH = 4
SPLIT = 4
ITEMS = 14


def one_hot(rows, cols, target):
    row = lax.broadcasted_iota(jnp.int32, (rows, cols), 0)
    col = lax.broadcasted_iota(jnp.int32, (rows, cols), 1)
    return (col == target(row)).astype(jnp.float32).astype(jnp.bfloat16)


def sigmoid(x):
    return 0.5 * jnp.tanh(0.5 * x) + 0.5


def matmul(a, b):
    return jnp.dot(a, b, preferred_element_type=jnp.float32)


def kernel(
    tokens_hbm, win_ref, wrec_ref, bias_hbm, table_hbm, out_ref,
    tokens_ref, bias_ref, table_ref, w, wperm, x, proj, s0, s1, obuf, r, cell, pt, back,
    local_sem, wsend, wrecv, xsend, xrecv, ssend, srecv, osend, orecv, gsend, grecv,
):
    groups = lax.axis_size("grp") // SPLIT
    ring = lax.axis_size("batch")
    q = lax.axis_index("grp")
    z = lax.axis_index("batch")
    g = q // SPLIT
    m = q % SPLIT
    mates = (m + 1 - 2 * (m % 2), (m + 2) % SPLIT, SPLIT - 1 - m)

    here = m // 2 * 2
    there = 2 - here

    def mate(d):
        return (g * SPLIT + mates[d], z)

    up = (q, (z + 1) % ring)
    down = (q, (z + ring - 1) % ring)

    barrier = pltpu.get_barrier_semaphore()
    for device in (up, down, mate(0), mate(1), mate(2)):
        pl.semaphore_signal(barrier, inc=1, device_id=device, device_id_type=MESH)

    @pl.loop(1, groups)
    def _(d):
        other = (g + d) % groups
        pl.semaphore_signal(
            barrier, inc=1, device_id=(other * SPLIT + m, z), device_id_type=MESH
        )

    loads = []
    for layer in range(2):
        for kind, ref in enumerate((win_ref, wrec_ref)):
            arr = 2 * layer + kind
            load = pltpu.make_async_copy(
                ref.at[layer], w.at[arr, pl.ds(z * 8, 8)], local_sem.at[arr]
            )
            load.start()
            loads.append(load)

    small = []
    for n, (ref, copy) in enumerate(
        ((tokens_hbm, tokens_ref), (bias_hbm, bias_ref), (table_hbm, table_ref))
    ):
        load = pltpu.make_async_copy(ref, copy, local_sem.at[4 + n])
        load.start()
        small.append(load)

    def item(n, way, came):
        arr, j = n // ITEMS, n % ITEMS
        hop, piece = j // DEPTH, j % DEPTH
        if way == 0:
            origin = (z + 2 * ring - hop - came) % ring
            device = up
        else:
            piece = (piece + DEPTH // 2) % DEPTH
            origin = (z + hop + came) % ring
            device = down
        view = w.at[arr, pl.ds(origin * 8 + piece * 2, 2)]
        return pltpu.make_async_remote_copy(
            src_ref=view, dst_ref=view, send_sem=wsend.at[n, way], recv_sem=wrecv.at[n, way],
            device_id=device, device_id_type=MESH,
        )

    def tick(n, more=True):
        for way in range(2):
            item(n, way, 1).wait_recv()
            if more:
                item(n + DEPTH, way, 0).start()
            item(n, way, 0).wait_send()

    def state_copy(states, layer, t, h, d, owner):
        view = states.at[t, h, owner]
        return pltpu.make_async_remote_copy(
            src_ref=view, dst_ref=view,
            send_sem=ssend.at[layer, t, h, d], recv_sem=srecv.at[layer, t, h, d],
            device_id=mate(d), device_id_type=MESH,
        )

    def input_copy(d, owner):
        view = x.at[owner]
        return pltpu.make_async_remote_copy(
            src_ref=view, dst_ref=view, send_sem=xsend.at[d], recv_sem=xrecv.at[d],
            device_id=mate(d), device_id_type=MESH,
        )

    def mixed_copy(p, d, owner):
        view = r.at[p, owner]
        return pltpu.make_async_remote_copy(
            src_ref=view, dst_ref=view, send_sem=gsend.at[p, d], recv_sem=grecv.at[p, d],
            device_id=mate(d), device_id_type=MESH,
        )

    def shuffled_all(p):
        return pltpu.make_async_remote_copy(
            src_ref=obuf.at[p, pl.ds(0, groups - 1)], dst_ref=r.at[p, m, pl.ds(0, groups - 1)],
            send_sem=osend.at[p], recv_sem=orecv.at[p], device_id=mate(0), device_id_type=MESH,
        )

    for load in loads:
        load.wait()
    pl.semaphore_wait(barrier, 5 + groups - 1)
    for n in range(DEPTH):
        for way in range(2):
            item(n, way, 0).start()

    for load in small:
        load.wait()

    rows = tokens_ref.shape[0]
    steps = proj.shape[0]
    seqs = rows // steps
    half = seqs // 2
    order = one_hot(rows, rows, lambda a: (a & (seqs - 1)) * steps + (a >> seqs.bit_length() - 1))
    x[m] = matmul(order, tokens_ref[...]).astype(jnp.bfloat16)
    for d in (2, 1, 0):
        input_copy(d, m).start()
    back[...] = one_hot(rows, rows, lambda a: (a & (steps - 1)) * seqs + (a >> steps.bit_length() - 1))

    lanes = 128
    per_row = lanes // 4
    odd = q // per_row
    row = lax.broadcasted_iota(jnp.int32, (lanes, lanes), 0)
    col = lax.broadcasted_iota(jnp.int32, (lanes, lanes), 1)
    mine = ((col >> 2) == q % per_row) & ((row & 1) == odd)
    entries = jnp.where(mine, table_ref[...] - q * 256, 0).astype(jnp.float32).astype(jnp.bfloat16)
    spread = matmul(one_hot(256, lanes, lambda a: (a >> 2) * 2 + odd), entries)
    row = lax.broadcasted_iota(jnp.int32, (256, lanes), 0)
    col = lax.broadcasted_iota(jnp.int32, (256, lanes), 1)
    wanted = col == (q % per_row) * 4 + (row & 3)
    picked = jnp.sum(jnp.where(wanted, spread, 0.0), axis=1, keepdims=True)
    channel = lax.broadcasted_iota(jnp.int32, (256, 256), 1).astype(jnp.float32)
    pt[...] = jnp.where(channel == picked, 1.0, 0.0).astype(jnp.bfloat16)

    def rows_of(arr, i):
        return w.at[arr, pl.ds(i * 16, 16)]

    @pl.loop(0, ITEMS)
    def _(n):
        tick(n)

    for d in range(3):
        input_copy(d, mates[d]).wait_recv()
        input_copy(d, m).wait_send()

    @pl.loop(0, 4)
    def _(c):
        cols = pl.ds(pl.multiple_of(c * 256, 256), 256)
        total = bias_ref[0:1, cols]
        for i in range(SPLIT):
            total = total + matmul(x[i], w[0, pl.ds(i * 16, 16), :, cols].reshape(256, 256))
        proj[:, :, :, cols] = total.reshape(steps, 2, half, 256)
        tick(ITEMS + c)

    def update(gate, states, layer, t, h, first=False):
        ingate = sigmoid(gate(0))
        cellgate = jnp.tanh(gate(2))
        now = ingate * cellgate
        if not first:
            now = now + sigmoid(gate(1)) * cell[h]
        outgate = sigmoid(gate(3))
        cell[h] = now
        states[t, h, m] = (outgate * jnp.tanh(now)).astype(jnp.bfloat16)

    def send_state(states, layer, t, h):
        for d in (1, 2, 0):
            state_copy(states, layer, t, h, d, m).start()

    def start(states, layer):
        for h in range(2):
            update(lambda k: proj[0, h, :, k * 256 : k * 256 + 256], states, layer, 0, h, first=True)
            send_state(states, layer, 0, h)

    def step(states, layer, t, h):
        arr = 2 * layer + 1

        def pair(first):
            both = [states[t - 1, h, first + i] for i in range(2)]
            return jnp.concatenate(both, axis=1)

        def product(lhs, first, k):
            cols = slice(k * 256, k * 256 + 256)
            return matmul(lhs, w[arr, pl.ds(first * 16, 32), :, cols].reshape(512, 256))

        state_copy(states, layer, t - 1, h, 0, mates[0]).wait_recv()
        lhs = pair(here)
        near = [
            proj[t, h, :, k * 256 : k * 256 + 256] + product(lhs, here, k) for k in range(4)
        ]
        for d in (1, 2):
            state_copy(states, layer, t - 1, h, d, mates[d]).wait_recv()
        lhs = pair(there)
        update(lambda k: near[k] + product(lhs, there, k), states, layer, t, h)

        @pl.when(t < steps - 1)
        def _():
            send_state(states, layer, t, h)

        for d in range(3):
            state_copy(states, layer, t - 1, h, d, m).wait_send()

    def forward(p):
        shuffled_all(p).wait_recv()
        for d in range(3):
            mixed_copy(p, d, m).start()

    start(s0, 0)

    @pl.loop(ITEMS + 4, 2 * ITEMS)
    def _(n):
        tick(n)

    @pl.loop(1, steps)
    def _(t):
        p = t // 2
        n = 2 * ITEMS + 3 * (t - 1)
        step(s0, 0, t, 0)
        tick(n)
        step(s0, 0, t, 1)
        tick(n + 1)

        @pl.when(t % 2 == 1)
        def _():
            pair = jnp.concatenate([s0[t - 1 + h // 2, h % 2, m] for h in range(4)], axis=0)
            moved = lax.dot_general(
                pt[...], pair, (((1,), (1,)), ((), ())), preferred_element_type=jnp.float32
            )
            obuf[p] = moved.astype(jnp.bfloat16).reshape(groups, 16, 128)
            r[p, m, g] = obuf[p, g]

            @pl.loop(1, groups)
            def _(d):
                other = (g + d) % groups
                pltpu.make_async_remote_copy(
                    src_ref=obuf.at[p, other], dst_ref=r.at[p, m, g],
                    send_sem=osend.at[p], recv_sem=orecv.at[p],
                    device_id=(other * SPLIT + m, z), device_id_type=MESH,
                ).start()

        @pl.when(t % 2 == 0)
        def _():
            forward(p - 1)

        tick(n + 2)

    swap = one_hot(64, 64, lambda a: ((a >> 2) & 3) * 16 + (a >> 4) * 4 + (a & 3))

    @pl.loop(0, groups)
    def _(i):
        block = jnp.concatenate([w[2, j * 16 + i] for j in range(SPLIT)], axis=0)
        block = matmul(swap, block).astype(jnp.bfloat16).reshape(SPLIT, 16, 1024)
        for j in range(SPLIT):
            wperm[j * 16 + i] = block[j]

        @pl.when(i % 8 == 7)
        def _():
            tick(4 * ITEMS - 7 + i // 8)

    tick(4 * ITEMS - 5)
    forward(steps // 2 - 1)

    @pl.loop(0, steps // 2)
    def _(p):
        shuffled_all(p).wait_send()
        for d in range(3):
            mixed_copy(p, d, mates[d]).wait_recv()
            mixed_copy(p, d, m).wait_send()
        total = lax.dot_general(
            r[p].reshape(1024, 128), wperm[...].reshape(1024, 1024),
            (((0,), (0,)), ((), ())), preferred_element_type=jnp.float32,
        )
        proj[pl.ds(2 * p, 2)] = (total + bias_ref[1:2, :]).reshape(2, 2, half, 1024)

    start(s1, 1)

    for n in range(4 * ITEMS - DEPTH, 4 * ITEMS):
        tick(n, False)

    @pl.loop(1, steps)
    def _(t):
        for h in range(2):
            step(s1, 1, t, h)

    states = jnp.concatenate([s1[h // 2, h % 2, m] for h in range(2 * steps)], axis=0)
    out_ref[...] = matmul(back[...], states).astype(jnp.bfloat16)


def local(tokens, input_weights, recur_weights, biases, shuffle):
    seqs, steps, units = tokens.shape
    depth = input_weights.shape[1]
    bf16 = jnp.bfloat16
    vmem = pl.BlockSpec(memory_space=pltpu.VMEM)
    hbm = pl.BlockSpec(memory_space=pl.ANY)
    dma = pltpu.SemaphoreType.DMA
    pairs = steps // 2
    out = pl.pallas_call(
        kernel,
        out_shape=jax.ShapeDtypeStruct((seqs * steps, units), bf16),
        in_specs=[hbm] * 5,
        out_specs=vmem,
        scratch_shapes=[
            pltpu.VMEM((seqs * steps, units), bf16),
            pltpu.VMEM((2, 1024), jnp.float32),
            pltpu.VMEM((128, 128), jnp.int32),
            pltpu.VMEM((4, 64, 16, 1024), bf16),
            pltpu.VMEM((64, 16, 1024), bf16),
            pltpu.VMEM((SPLIT, seqs * steps, units), bf16),
            pltpu.VMEM((steps, 2, seqs // 2, 1024), jnp.float32),
            pltpu.VMEM((steps, 2, SPLIT, seqs // 2, units), bf16),
            pltpu.VMEM((steps, 2, SPLIT, seqs // 2, units), bf16),
            pltpu.VMEM((pairs, 16, 16, 128), bf16),
            pltpu.VMEM((pairs, SPLIT, 16, 16, 128), bf16),
            pltpu.VMEM((2, seqs // 2, units), jnp.float32),
            pltpu.VMEM((256, 256), bf16),
            pltpu.VMEM((512, 512), bf16),
            dma((7,)),
            dma((4 * ITEMS, 2)),
            dma((4 * ITEMS, 2)),
            dma((3,)),
            dma((3,)),
            dma((2, steps, 2, 3)),
            dma((2, steps, 2, 3)),
            dma((pairs,)),
            dma((pairs,)),
            dma((pairs, 3)),
            dma((pairs, 3)),
        ],
        compiler_params=pltpu.CompilerParams(
            collective_id=0, has_side_effects=True, vmem_limit_bytes=63 * 1024 * 1024
        ),
    )(
        tokens.reshape(seqs * steps, units),
        input_weights.reshape(2, depth // 16, 16, 1024),
        recur_weights.reshape(2, depth // 16, 16, 1024),
        biases,
        shuffle.reshape(128, 128),
    )
    return out.reshape(seqs, steps, units)


def solution(mesh):
    return jax.shard_map(
        local,
        mesh=mesh,
        in_specs=(
            P("batch", None, "grp"),
            P(None, "batch", "grp"),
            P(None, "batch", "grp"),
            P(None, "grp"),
            P(),
        ),
        out_specs=P("batch", None, "grp"),
        check_vma=False,
    )
```

```python
import jax
import jax.numpy as jnp
from jax import lax
from jax.experimental import pallas as pl
from jax.experimental.pallas import tpu as pltpu
from jax.sharding import PartitionSpec as P

MESH = pl.DeviceIdType.MESH
DEPTH = 4
SPLIT = 4
ITEMS = 14


def one_hot(rows, cols, target):
    row = lax.broadcasted_iota(jnp.int32, (rows, cols), 0)
    col = lax.broadcasted_iota(jnp.int32, (rows, cols), 1)
    return (col == target(row)).astype(jnp.float32).astype(jnp.bfloat16)


def sigmoid(x):
    return 0.5 * jnp.tanh(0.5 * x) + 0.5


def matmul(a, b):
    return jnp.dot(a, b, preferred_element_type=jnp.float32)


def kernel(
    tokens_hbm, win_ref, wrec_ref, bias_hbm, table_hbm, out_ref,
    tokens_ref, bias_ref, table_ref, w, wperm, x, proj, s0, s1, obuf, r, cell, pt, back,
    local_sem, wsend, wrecv, xsend, xrecv, ssend, srecv, osend, orecv, gsend, grecv,
):
    groups = lax.axis_size("grp") // SPLIT
    ring = lax.axis_size("batch")
    q = lax.axis_index("grp")
    z = lax.axis_index("batch")
    g = q // SPLIT
    m = q % SPLIT
    mates = (m + 1 - 2 * (m % 2), (m + 2) % SPLIT, SPLIT - 1 - m)

    here = m // 2 * 2
    there = 2 - here

    def mate(d):
        return (g * SPLIT + mates[d], z)

    up = (q, (z + 1) % ring)
    down = (q, (z + ring - 1) % ring)

    barrier = pltpu.get_barrier_semaphore()
    for device in (up, down, mate(0), mate(1), mate(2)):
        pl.semaphore_signal(barrier, inc=1, device_id=device, device_id_type=MESH)

    @pl.loop(1, groups)
    def _(d):
        other = (g + d) % groups
        pl.semaphore_signal(
            barrier, inc=1, device_id=(other * SPLIT + m, z), device_id_type=MESH
        )

    loads = []
    for layer in range(2):
        for kind, ref in enumerate((win_ref, wrec_ref)):
            arr = 2 * layer + kind
            load = pltpu.make_async_copy(
                ref.at[layer], w.at[arr, pl.ds(z * 8, 8)], local_sem.at[arr]
            )
            load.start()
            loads.append(load)

    small = []
    for n, (ref, copy) in enumerate(
        ((tokens_hbm, tokens_ref), (bias_hbm, bias_ref), (table_hbm, table_ref))
    ):
        load = pltpu.make_async_copy(ref, copy, local_sem.at[4 + n])
        load.start()
        small.append(load)

    def item(n, way, came):
        arr, j = n // ITEMS, n % ITEMS
        hop, piece = j // DEPTH, j % DEPTH
        if way == 0:
            origin = (z + 2 * ring - hop - came) % ring
            device = up
        else:
            piece = (piece + DEPTH // 2) % DEPTH
            origin = (z + hop + came) % ring
            device = down
        view = w.at[arr, pl.ds(origin * 8 + piece * 2, 2)]
        return pltpu.make_async_remote_copy(
            src_ref=view, dst_ref=view, send_sem=wsend.at[n, way], recv_sem=wrecv.at[n, way],
            device_id=device, device_id_type=MESH,
        )

    def tick(n, more=True):
        for way in range(2):
            item(n, way, 1).wait_recv()
            if more:
                item(n + DEPTH, way, 0).start()
            item(n, way, 0).wait_send()

    def state_copy(states, layer, t, h, d, owner):
        view = states.at[t, h, owner]
        return pltpu.make_async_remote_copy(
            src_ref=view, dst_ref=view,
            send_sem=ssend.at[layer, t, h, d], recv_sem=srecv.at[layer, t, h, d],
            device_id=mate(d), device_id_type=MESH,
        )

    def input_copy(d, owner):
        view = x.at[owner]
        return pltpu.make_async_remote_copy(
            src_ref=view, dst_ref=view, send_sem=xsend.at[d], recv_sem=xrecv.at[d],
            device_id=mate(d), device_id_type=MESH,
        )

    def mixed_copy(p, d, owner):
        view = r.at[p, owner]
        return pltpu.make_async_remote_copy(
            src_ref=view, dst_ref=view, send_sem=gsend.at[p, d], recv_sem=grecv.at[p, d],
            device_id=mate(d), device_id_type=MESH,
        )

    def shuffled_all(p):
        return pltpu.make_async_remote_copy(
            src_ref=obuf.at[p, pl.ds(0, groups - 1)], dst_ref=r.at[p, m, pl.ds(0, groups - 1)],
            send_sem=osend.at[p], recv_sem=orecv.at[p], device_id=mate(0), device_id_type=MESH,
        )

    for load in loads:
        load.wait()
    pl.semaphore_wait(barrier, 5 + groups - 1)
    for n in range(DEPTH):
        for way in range(2):
            item(n, way, 0).start()

    for load in small:
        load.wait()

    rows = tokens_ref.shape[0]
    steps = proj.shape[0]
    seqs = rows // steps
    half = seqs // 2
    order = one_hot(rows, rows, lambda a: (a & (seqs - 1)) * steps + (a >> seqs.bit_length() - 1))
    x[m] = matmul(order, tokens_ref[...]).astype(jnp.bfloat16)
    for d in (2, 1, 0):
        input_copy(d, m).start()
    back[...] = one_hot(rows, rows, lambda a: (a & (steps - 1)) * seqs + (a >> steps.bit_length() - 1))

    lanes = 128
    per_row = lanes // 4
    odd = q // per_row
    row = lax.broadcasted_iota(jnp.int32, (lanes, lanes), 0)
    col = lax.broadcasted_iota(jnp.int32, (lanes, lanes), 1)
    mine = ((col >> 2) == q % per_row) & ((row & 1) == odd)
    entries = jnp.where(mine, table_ref[...] - q * 256, 0).astype(jnp.float32).astype(jnp.bfloat16)
    spread = matmul(one_hot(256, lanes, lambda a: (a >> 2) * 2 + odd), entries)
    row = lax.broadcasted_iota(jnp.int32, (256, lanes), 0)
    col = lax.broadcasted_iota(jnp.int32, (256, lanes), 1)
    wanted = col == (q % per_row) * 4 + (row & 3)
    picked = jnp.sum(jnp.where(wanted, spread, 0.0), axis=1, keepdims=True)
    channel = lax.broadcasted_iota(jnp.int32, (256, 256), 1).astype(jnp.float32)
    pt[...] = jnp.where(channel == picked, 1.0, 0.0).astype(jnp.bfloat16)

    def rows_of(arr, i):
        return w.at[arr, pl.ds(i * 16, 16)]

    @pl.loop(0, ITEMS)
    def _(n):
        tick(n)

    for d in range(3):
        input_copy(d, mates[d]).wait_recv()
        input_copy(d, m).wait_send()

    @pl.loop(0, 4)
    def _(c):
        cols = pl.ds(pl.multiple_of(c * 256, 256), 256)
        total = bias_ref[0:1, cols]
        for i in range(SPLIT):
            total = total + matmul(x[i], w[0, pl.ds(i * 16, 16), :, cols].reshape(256, 256))
        proj[:, :, :, cols] = total.reshape(steps, 2, half, 256)
        tick(ITEMS + c)

    def update(gate, states, layer, t, h, first=False):
        ingate = sigmoid(gate(0))
        cellgate = jnp.tanh(gate(2))
        now = ingate * cellgate
        if not first:
            now = now + sigmoid(gate(1)) * cell[h]
        outgate = sigmoid(gate(3))
        cell[h] = now
        states[t, h, m] = (outgate * jnp.tanh(now)).astype(jnp.bfloat16)

    def send_state(states, layer, t, h):
        for d in (1, 2, 0):
            state_copy(states, layer, t, h, d, m).start()

    def start(states, layer):
        for h in range(2):
            update(lambda k: proj[0, h, :, k * 256 : k * 256 + 256], states, layer, 0, h, first=True)
            send_state(states, layer, 0, h)

    def step(states, layer, t, h):
        arr = 2 * layer + 1

        def pair(first):
            both = [states[t - 1, h, first + i] for i in range(2)]
            return jnp.concatenate(both, axis=1)

        def product(first):
            return matmul(pair(first), w[arr, pl.ds(first * 16, 32)].reshape(512, 1024))

        state_copy(states, layer, t - 1, h, 0, mates[0]).wait_recv()
        pre = proj[t, h] + product(here)
        for d in (1, 2):
            state_copy(states, layer, t - 1, h, d, mates[d]).wait_recv()
        pre = pre + product(there)
        update(lambda k: pre[:, k * 256 : k * 256 + 256], states, layer, t, h)

        @pl.when(t < steps - 1)
        def _():
            send_state(states, layer, t, h)

        for d in range(3):
            state_copy(states, layer, t - 1, h, d, m).wait_send()

    def forward(p):
        shuffled_all(p).wait_recv()
        for d in range(3):
            mixed_copy(p, d, m).start()

    start(s0, 0)

    @pl.loop(ITEMS + 4, 2 * ITEMS)
    def _(n):
        tick(n)

    @pl.loop(1, steps)
    def _(t):
        p = t // 2
        n = 2 * ITEMS + 3 * (t - 1)
        step(s0, 0, t, 0)
        tick(n)
        step(s0, 0, t, 1)
        tick(n + 1)

        @pl.when(t % 2 == 1)
        def _():
            pair = jnp.concatenate([s0[t - 1 + h // 2, h % 2, m] for h in range(4)], axis=0)
            moved = lax.dot_general(
                pt[...], pair, (((1,), (1,)), ((), ())), preferred_element_type=jnp.float32
            )
            obuf[p] = moved.astype(jnp.bfloat16).reshape(groups, 16, 128)
            r[p, m, g] = obuf[p, g]

            @pl.loop(1, groups)
            def _(d):
                other = (g + d) % groups
                pltpu.make_async_remote_copy(
                    src_ref=obuf.at[p, other], dst_ref=r.at[p, m, g],
                    send_sem=osend.at[p], recv_sem=orecv.at[p],
                    device_id=(other * SPLIT + m, z), device_id_type=MESH,
                ).start()

        @pl.when(t % 2 == 0)
        def _():
            forward(p - 1)

        tick(n + 2)

    swap = one_hot(64, 64, lambda a: ((a >> 2) & 3) * 16 + (a >> 4) * 4 + (a & 3))

    @pl.loop(0, groups)
    def _(i):
        block = jnp.concatenate([w[2, j * 16 + i] for j in range(SPLIT)], axis=0)
        block = matmul(swap, block).astype(jnp.bfloat16).reshape(SPLIT, 16, 1024)
        for j in range(SPLIT):
            wperm[j * 16 + i] = block[j]

        @pl.when(i % 8 == 7)
        def _():
            tick(4 * ITEMS - 7 + i // 8)

    tick(4 * ITEMS - 5)
    forward(steps // 2 - 1)

    @pl.loop(0, steps // 2)
    def _(p):
        shuffled_all(p).wait_send()
        for d in range(3):
            mixed_copy(p, d, mates[d]).wait_recv()
            mixed_copy(p, d, m).wait_send()
        total = lax.dot_general(
            r[p].reshape(1024, 128), wperm[...].reshape(1024, 1024),
            (((0,), (0,)), ((), ())), preferred_element_type=jnp.float32,
        )
        proj[pl.ds(2 * p, 2)] = (total + bias_ref[1:2, :]).reshape(2, 2, half, 1024)

    start(s1, 1)

    for n in range(4 * ITEMS - DEPTH, 4 * ITEMS):
        tick(n, False)

    @pl.loop(1, steps)
    def _(t):
        for h in range(2):
            step(s1, 1, t, h)

    states = jnp.concatenate([s1[h // 2, h % 2, m] for h in range(2 * steps)], axis=0)
    out_ref[...] = matmul(back[...], states).astype(jnp.bfloat16)


def local(tokens, input_weights, recur_weights, biases, shuffle):
    seqs, steps, units = tokens.shape
    depth = input_weights.shape[1]
    bf16 = jnp.bfloat16
    vmem = pl.BlockSpec(memory_space=pltpu.VMEM)
    hbm = pl.BlockSpec(memory_space=pl.ANY)
    dma = pltpu.SemaphoreType.DMA
    pairs = steps // 2
    out = pl.pallas_call(
        kernel,
        out_shape=jax.ShapeDtypeStruct((seqs * steps, units), bf16),
        in_specs=[hbm] * 5,
        out_specs=vmem,
        scratch_shapes=[
            pltpu.VMEM((seqs * steps, units), bf16),
            pltpu.VMEM((2, 1024), jnp.float32),
            pltpu.VMEM((128, 128), jnp.int32),
            pltpu.VMEM((4, 64, 16, 1024), bf16),
            pltpu.VMEM((64, 16, 1024), bf16),
            pltpu.VMEM((SPLIT, seqs * steps, units), bf16),
            pltpu.VMEM((steps, 2, seqs // 2, 1024), jnp.float32),
            pltpu.VMEM((steps, 2, SPLIT, seqs // 2, units), bf16),
            pltpu.VMEM((steps, 2, SPLIT, seqs // 2, units), bf16),
            pltpu.VMEM((pairs, 16, 16, 128), bf16),
            pltpu.VMEM((pairs, SPLIT, 16, 16, 128), bf16),
            pltpu.VMEM((2, seqs // 2, units), jnp.float32),
            pltpu.VMEM((256, 256), bf16),
            pltpu.VMEM((512, 512), bf16),
            dma((7,)),
            dma((4 * ITEMS, 2)),
            dma((4 * ITEMS, 2)),
            dma((3,)),
            dma((3,)),
            dma((2, steps, 2, 3)),
            dma((2, steps, 2, 3)),
            dma((pairs,)),
            dma((pairs,)),
            dma((pairs, 3)),
            dma((pairs, 3)),
        ],
        compiler_params=pltpu.CompilerParams(
            collective_id=0, has_side_effects=True, vmem_limit_bytes=63 * 1024 * 1024
        ),
    )(
        tokens.reshape(seqs * steps, units),
        input_weights.reshape(2, depth // 16, 16, 1024),
        recur_weights.reshape(2, depth // 16, 16, 1024),
        biases,
        shuffle.reshape(128, 128),
    )
    return out.reshape(seqs, steps, units)


def solution(mesh):
    return jax.shard_map(
        local,
        mesh=mesh,
        in_specs=(
            P("batch", None, "grp"),
            P(None, "batch", "grp"),
            P(None, "batch", "grp"),
            P(None, "grp"),
            P(),
        ),
        out_specs=P("batch", None, "grp"),
        check_vma=False,
    )
```

```python
import jax
import jax.numpy as jnp
from jax import lax
from jax.experimental import pallas as pl
from jax.experimental.pallas import tpu as pltpu
from jax.sharding import PartitionSpec as P

MESH = pl.DeviceIdType.MESH
DEPTH = 4
SPLIT = 4
PARTS = 1
ITEMS = 14


def one_hot(rows, cols, target):
    row = lax.broadcasted_iota(jnp.int32, (rows, cols), 0)
    col = lax.broadcasted_iota(jnp.int32, (rows, cols), 1)
    return (col == target(row)).astype(jnp.float32).astype(jnp.bfloat16)


def sigmoid(x):
    return 0.5 * jnp.tanh(0.5 * x) + 0.5


def matmul(a, b):
    return jnp.dot(a, b, preferred_element_type=jnp.float32)


def kernel(
    tokens_hbm, win_ref, wrec_ref, bias_hbm, table_hbm, out_ref,
    tokens_ref, bias_ref, table_ref, w, wperm, x, proj, s0, s1, obuf, r, cell, pt, back,
    local_sem, wsend, wrecv, xsend, xrecv, ssend, srecv, osend, orecv, gsend, grecv,
):
    groups = lax.axis_size("grp") // SPLIT
    ring = lax.axis_size("batch")
    q = lax.axis_index("grp")
    z = lax.axis_index("batch")
    g = q // SPLIT
    m = q % SPLIT
    mates = (m + 1 - 2 * (m % 2), (m + 2) % SPLIT, SPLIT - 1 - m)

    here = m // 2 * 2
    there = 2 - here

    def mate(d):
        return (g * SPLIT + mates[d], z)

    up = (q, (z + 1) % ring)
    down = (q, (z + ring - 1) % ring)

    barrier = pltpu.get_barrier_semaphore()
    for device in (up, down, mate(0), mate(1), mate(2)):
        pl.semaphore_signal(barrier, inc=1, device_id=device, device_id_type=MESH)

    @pl.loop(1, groups)
    def _(d):
        other = (g + d) % groups
        pl.semaphore_signal(
            barrier, inc=1, device_id=(other * SPLIT + m, z), device_id_type=MESH
        )

    loads = []
    for layer in range(2):
        for kind, ref in enumerate((win_ref, wrec_ref)):
            arr = 2 * layer + kind
            load = pltpu.make_async_copy(
                ref.at[layer], w.at[arr, pl.ds(z * 8, 8)], local_sem.at[arr]
            )
            load.start()
            loads.append(load)

    small = []
    for n, (ref, copy) in enumerate(
        ((tokens_hbm, tokens_ref), (bias_hbm, bias_ref), (table_hbm, table_ref))
    ):
        load = pltpu.make_async_copy(ref, copy, local_sem.at[4 + n])
        load.start()
        small.append(load)

    def item(n, way, came):
        arr, j = n // ITEMS, n % ITEMS
        hop, piece = j // DEPTH, j % DEPTH
        if way == 0:
            origin = (z + 2 * ring - hop - came) % ring
            device = up
        else:
            piece = (piece + DEPTH // 2) % DEPTH
            origin = (z + hop + came) % ring
            device = down
        view = w.at[arr, pl.ds(origin * 8 + piece * 2, 2)]
        return pltpu.make_async_remote_copy(
            src_ref=view, dst_ref=view, send_sem=wsend.at[n, way], recv_sem=wrecv.at[n, way],
            device_id=device, device_id_type=MESH,
        )

    def tick(n, more=True):
        for way in range(2):
            item(n, way, 1).wait_recv()
            if more:
                item(n + DEPTH, way, 0).start()
            item(n, way, 0).wait_send()

    def state_copy(states, layer, t, h, d, owner):
        view = states.at[t, h, owner]
        return pltpu.make_async_remote_copy(
            src_ref=view, dst_ref=view,
            send_sem=ssend.at[layer, t, h, d], recv_sem=srecv.at[layer, t, h, d],
            device_id=mate(d), device_id_type=MESH,
        )

    def input_copy(d, owner):
        view = x.at[owner]
        return pltpu.make_async_remote_copy(
            src_ref=view, dst_ref=view, send_sem=xsend.at[d], recv_sem=xrecv.at[d],
            device_id=mate(d), device_id_type=MESH,
        )

    def mixed_copy(p, d, owner):
        view = r.at[p, owner]
        return pltpu.make_async_remote_copy(
            src_ref=view, dst_ref=view, send_sem=gsend.at[p, d], recv_sem=grecv.at[p, d],
            device_id=mate(d), device_id_type=MESH,
        )

    def shuffled_all(p):
        return pltpu.make_async_remote_copy(
            src_ref=obuf.at[p, pl.ds(0, groups - 1)], dst_ref=r.at[p, m, pl.ds(0, groups - 1)],
            send_sem=osend.at[p], recv_sem=orecv.at[p], device_id=mate(0), device_id_type=MESH,
        )

    for load in loads:
        load.wait()
    pl.semaphore_wait(barrier, 5 + groups - 1)
    for n in range(DEPTH):
        for way in range(2):
            item(n, way, 0).start()

    for load in small:
        load.wait()

    rows = tokens_ref.shape[0]
    steps = proj.shape[0]
    seqs = rows // steps
    part = seqs // PARTS
    order = one_hot(rows, rows, lambda a: (a & (seqs - 1)) * steps + (a >> seqs.bit_length() - 1))
    x[m] = matmul(order, tokens_ref[...]).astype(jnp.bfloat16)
    for d in (2, 1, 0):
        input_copy(d, m).start()
    back[...] = one_hot(rows, rows, lambda a: (a & (steps - 1)) * seqs + (a >> steps.bit_length() - 1))

    lanes = 128
    per_row = lanes // 4
    odd = q // per_row
    row = lax.broadcasted_iota(jnp.int32, (lanes, lanes), 0)
    col = lax.broadcasted_iota(jnp.int32, (lanes, lanes), 1)
    mine = ((col >> 2) == q % per_row) & ((row & 1) == odd)
    entries = jnp.where(mine, table_ref[...] - q * 256, 0).astype(jnp.float32).astype(jnp.bfloat16)
    spread = matmul(one_hot(256, lanes, lambda a: (a >> 2) * 2 + odd), entries)
    row = lax.broadcasted_iota(jnp.int32, (256, lanes), 0)
    col = lax.broadcasted_iota(jnp.int32, (256, lanes), 1)
    wanted = col == (q % per_row) * 4 + (row & 3)
    picked = jnp.sum(jnp.where(wanted, spread, 0.0), axis=1, keepdims=True)
    channel = lax.broadcasted_iota(jnp.int32, (256, 256), 1).astype(jnp.float32)
    pt[...] = jnp.where(channel == picked, 1.0, 0.0).astype(jnp.bfloat16)

    def rows_of(arr, i):
        return w.at[arr, pl.ds(i * 16, 16)]

    @pl.loop(0, ITEMS)
    def _(n):
        tick(n)

    for d in range(3):
        input_copy(d, mates[d]).wait_recv()
        input_copy(d, m).wait_send()

    @pl.loop(0, 4)
    def _(c):
        cols = pl.ds(pl.multiple_of(c * 256, 256), 256)
        total = bias_ref[0:1, cols]
        for i in range(SPLIT):
            total = total + matmul(x[i], w[0, pl.ds(i * 16, 16), :, cols].reshape(256, 256))
        proj[:, :, :, cols] = total.reshape(steps, PARTS, part, 256)
        tick(ITEMS + c)

    def update(gate, states, layer, t, h, first=False):
        ingate = sigmoid(gate(0))
        cellgate = jnp.tanh(gate(2))
        now = ingate * cellgate
        if not first:
            now = now + sigmoid(gate(1)) * cell[h]
        outgate = sigmoid(gate(3))
        cell[h] = now
        states[t, h, m] = (outgate * jnp.tanh(now)).astype(jnp.bfloat16)

    def send_state(states, layer, t, h):
        for d in (1, 2, 0):
            state_copy(states, layer, t, h, d, m).start()

    def start(states, layer):
        for h in range(PARTS):
            update(lambda k: proj[0, h, :, k * 256 : k * 256 + 256], states, layer, 0, h, first=True)
            send_state(states, layer, 0, h)

    def step(states, layer, t, h):
        arr = 2 * layer + 1

        def pair(first):
            both = [states[t - 1, h, first + i] for i in range(2)]
            return jnp.concatenate(both, axis=1)

        def product(first):
            return matmul(pair(first), w[arr, pl.ds(first * 16, 32)].reshape(512, 1024))

        state_copy(states, layer, t - 1, h, 0, mates[0]).wait_recv()
        pre = proj[t, h] + product(here)
        for d in (1, 2):
            state_copy(states, layer, t - 1, h, d, mates[d]).wait_recv()
        pre = pre + product(there)
        update(lambda k: pre[:, k * 256 : k * 256 + 256], states, layer, t, h)

        @pl.when(t < steps - 1)
        def _():
            send_state(states, layer, t, h)

        for d in range(3):
            state_copy(states, layer, t - 1, h, d, m).wait_send()

    def forward(p):
        shuffled_all(p).wait_recv()
        for d in range(3):
            mixed_copy(p, d, m).start()

    start(s0, 0)

    @pl.loop(ITEMS + 4, 2 * ITEMS)
    def _(n):
        tick(n)

    @pl.loop(1, steps)
    def _(t):
        p = t // 2
        n = 2 * ITEMS + 3 * (t - 1)
        step(s0, 0, t, 0)
        tick(n)
        for h in range(1, PARTS):
            step(s0, 0, t, h)
        tick(n + 1)

        @pl.when(t % 2 == 1)
        def _():
            pair = jnp.concatenate([s0[t - 1 + h // PARTS, h % PARTS, m] for h in range(2 * PARTS)], axis=0)
            moved = lax.dot_general(
                pt[...], pair, (((1,), (1,)), ((), ())), preferred_element_type=jnp.float32
            )
            obuf[p] = moved.astype(jnp.bfloat16).reshape(groups, 16, 128)
            r[p, m, g] = obuf[p, g]

            @pl.loop(1, groups)
            def _(d):
                other = (g + d) % groups
                pltpu.make_async_remote_copy(
                    src_ref=obuf.at[p, other], dst_ref=r.at[p, m, g],
                    send_sem=osend.at[p], recv_sem=orecv.at[p],
                    device_id=(other * SPLIT + m, z), device_id_type=MESH,
                ).start()

        @pl.when(t % 2 == 0)
        def _():
            forward(p - 1)

        tick(n + 2)

    swap = one_hot(64, 64, lambda a: ((a >> 2) & 3) * 16 + (a >> 4) * 4 + (a & 3))

    @pl.loop(0, groups)
    def _(i):
        block = jnp.concatenate([w[2, j * 16 + i] for j in range(SPLIT)], axis=0)
        block = matmul(swap, block).astype(jnp.bfloat16).reshape(SPLIT, 16, 1024)
        for j in range(SPLIT):
            wperm[j * 16 + i] = block[j]

        @pl.when(i % 8 == 7)
        def _():
            tick(4 * ITEMS - 7 + i // 8)

    tick(4 * ITEMS - 5)
    forward(steps // 2 - 1)

    def project_mixed(p):
        shuffled_all(p).wait_send()
        for d in range(3):
            mixed_copy(p, d, mates[d]).wait_recv()
            mixed_copy(p, d, m).wait_send()
        total = lax.dot_general(
            r[p].reshape(1024, 128), wperm[...].reshape(1024, 1024),
            (((0,), (0,)), ((), ())), preferred_element_type=jnp.float32,
        )
        proj[pl.ds(2 * p, 2)] = (total + bias_ref[1:2, :]).reshape(2, PARTS, part, 1024)

    @pl.loop(0, steps // 2 - 1)
    def _(p):
        project_mixed(p)

    start(s1, 1)

    for n in range(4 * ITEMS - DEPTH, 4 * ITEMS):
        tick(n, False)

    @pl.loop(1, steps)
    def _(t):
        for h in range(PARTS):
            step(s1, 1, t, h)

        @pl.when(t == 1)
        def _():
            project_mixed(steps // 2 - 1)

    states = jnp.concatenate([s1[h // PARTS, h % PARTS, m] for h in range(PARTS * steps)], axis=0)
    out_ref[...] = matmul(back[...], states).astype(jnp.bfloat16)


def local(tokens, input_weights, recur_weights, biases, shuffle):
    seqs, steps, units = tokens.shape
    depth = input_weights.shape[1]
    bf16 = jnp.bfloat16
    vmem = pl.BlockSpec(memory_space=pltpu.VMEM)
    hbm = pl.BlockSpec(memory_space=pl.ANY)
    dma = pltpu.SemaphoreType.DMA
    pairs = steps // 2
    out = pl.pallas_call(
        kernel,
        out_shape=jax.ShapeDtypeStruct((seqs * steps, units), bf16),
        in_specs=[hbm] * 5,
        out_specs=vmem,
        scratch_shapes=[
            pltpu.VMEM((seqs * steps, units), bf16),
            pltpu.VMEM((2, 1024), jnp.float32),
            pltpu.VMEM((128, 128), jnp.int32),
            pltpu.VMEM((4, 64, 16, 1024), bf16),
            pltpu.VMEM((64, 16, 1024), bf16),
            pltpu.VMEM((SPLIT, seqs * steps, units), bf16),
            pltpu.VMEM((steps, PARTS, seqs // PARTS, 1024), jnp.float32),
            pltpu.VMEM((steps, PARTS, SPLIT, seqs // PARTS, units), bf16),
            pltpu.VMEM((steps, PARTS, SPLIT, seqs // PARTS, units), bf16),
            pltpu.VMEM((pairs, 16, 16, 128), bf16),
            pltpu.VMEM((pairs, SPLIT, 16, 16, 128), bf16),
            pltpu.VMEM((PARTS, seqs // PARTS, units), jnp.float32),
            pltpu.VMEM((256, 256), bf16),
            pltpu.VMEM((512, 512), bf16),
            dma((7,)),
            dma((4 * ITEMS, 2)),
            dma((4 * ITEMS, 2)),
            dma((3,)),
            dma((3,)),
            dma((2, steps, PARTS, 3)),
            dma((2, steps, PARTS, 3)),
            dma((pairs,)),
            dma((pairs,)),
            dma((pairs, 3)),
            dma((pairs, 3)),
        ],
        compiler_params=pltpu.CompilerParams(
            collective_id=0, has_side_effects=True, vmem_limit_bytes=63 * 1024 * 1024
        ),
    )(
        tokens.reshape(seqs * steps, units),
        input_weights.reshape(2, depth // 16, 16, 1024),
        recur_weights.reshape(2, depth // 16, 16, 1024),
        biases,
        shuffle.reshape(128, 128),
    )
    return out.reshape(seqs, steps, units)


def solution(mesh):
    return jax.shard_map(
        local,
        mesh=mesh,
        in_specs=(
            P("batch", None, "grp"),
            P(None, "batch", "grp"),
            P(None, "batch", "grp"),
            P(None, "grp"),
            P(),
        ),
        out_specs=P("batch", None, "grp"),
        check_vma=False,
    )
```

```python
import jax
import jax.numpy as jnp
from jax import lax
from jax.experimental import pallas as pl
from jax.experimental.pallas import tpu as pltpu
from jax.sharding import PartitionSpec as P

MESH = pl.DeviceIdType.MESH
DEPTH = 4
SPLIT = 4
PARTS = 1
ITEMS = 14


def one_hot(rows, cols, target):
    row = lax.broadcasted_iota(jnp.int32, (rows, cols), 0)
    col = lax.broadcasted_iota(jnp.int32, (rows, cols), 1)
    return (col == target(row)).astype(jnp.float32).astype(jnp.bfloat16)


def sigmoid(x):
    return 0.5 * jnp.tanh(0.5 * x) + 0.5


def matmul(a, b):
    return jnp.dot(a, b, preferred_element_type=jnp.float32)


def kernel(
    tokens_hbm, win_ref, wrec_ref, bias_hbm, table_hbm, out_ref,
    tokens_ref, bias_ref, table_ref, w, wperm, x, proj, s0, s1, obuf, r, cell, pt,
    local_sem, wsend, wrecv, xsend, xrecv, ssend, srecv, osend, orecv, gsend, grecv, done,
):
    groups = lax.axis_size("grp") // SPLIT
    ring = lax.axis_size("batch")
    q = lax.axis_index("grp")
    z = lax.axis_index("batch")
    g = q // SPLIT
    m = q % SPLIT
    mates = (m + 1 - 2 * (m % 2), (m + 2) % SPLIT, SPLIT - 1 - m)

    here = m // 2 * 2

    def mate(d):
        return (g * SPLIT + mates[d], z)

    up = (q, (z + 1) % ring)
    down = (q, (z + ring - 1) % ring)

    loads = []
    for layer in range(2):
        for kind, ref in enumerate((win_ref, wrec_ref)):
            arr = 2 * layer + kind
            load = pltpu.make_async_copy(
                ref.at[layer], w.at[arr, pl.ds(z * 8, 8)], local_sem.at[arr]
            )
            load.start()
            loads.append(load)

    small = []
    for n, (ref, copy) in enumerate(
        ((tokens_hbm, tokens_ref), (bias_hbm, bias_ref), (table_hbm, table_ref))
    ):
        load = pltpu.make_async_copy(ref, copy, local_sem.at[4 + n])
        load.start()
        small.append(load)

    barrier = pltpu.get_barrier_semaphore()
    for device in (up, down, mate(0), mate(1), mate(2)):
        pl.semaphore_signal(barrier, inc=1, device_id=device, device_id_type=MESH)

    @pl.loop(1, groups)
    def _(d):
        other = (g + d) % groups
        pl.semaphore_signal(
            barrier, inc=1, device_id=(other * SPLIT + m, z), device_id_type=MESH
        )

    def item(n, way, came):
        arr, j = n // ITEMS, n % ITEMS
        hop, piece = j // DEPTH, j % DEPTH
        if way == 0:
            origin = (z + 2 * ring - hop - came) % ring
            device = up
        else:
            piece = (piece + DEPTH // 2) % DEPTH
            origin = (z + hop + came) % ring
            device = down
        view = w.at[arr, pl.ds(origin * 8 + piece * 2, 2)]
        return pltpu.make_async_remote_copy(
            src_ref=view, dst_ref=view, send_sem=wsend.at[n, way], recv_sem=wrecv.at[n, way],
            device_id=device, device_id_type=MESH,
        )

    def tick(n, more=True):
        for way in range(2):
            item(n, way, 1).wait_recv()
            if more:
                item(n + DEPTH, way, 0).start()
            item(n, way, 0).wait_send()

    def state_copy(states, layer, t, h, d, owner):
        view = states.at[t, h, owner]
        return pltpu.make_async_remote_copy(
            src_ref=view, dst_ref=view,
            send_sem=ssend.at[layer, t, h, d], recv_sem=srecv.at[layer, t, h, d],
            device_id=mate(d), device_id_type=MESH,
        )

    def input_copy(d, owner):
        view = x.at[owner]
        return pltpu.make_async_remote_copy(
            src_ref=view, dst_ref=view, send_sem=xsend.at[d], recv_sem=xrecv.at[d],
            device_id=mate(d), device_id_type=MESH,
        )

    def mixed_copy(p, d, owner):
        view = r.at[p, owner]
        return pltpu.make_async_remote_copy(
            src_ref=view, dst_ref=view, send_sem=gsend.at[p, d], recv_sem=grecv.at[p, d],
            device_id=mate(d), device_id_type=MESH,
        )

    def shuffled_all(p):
        return pltpu.make_async_remote_copy(
            src_ref=obuf.at[p, pl.ds(0, groups - 1)], dst_ref=r.at[p, m, pl.ds(0, groups - 1)],
            send_sem=osend.at[p], recv_sem=orecv.at[p], device_id=mate(0), device_id_type=MESH,
        )

    loads[0].wait()
    pl.semaphore_wait(barrier, 5 + groups - 1)
    for n in range(DEPTH):
        for way in range(2):
            item(n, way, 0).start()

    for load in small + loads[1:]:
        load.wait()

    rows = tokens_ref.shape[0]
    steps = proj.shape[0]
    seqs = rows // steps
    part = seqs // PARTS
    order = one_hot(rows, rows, lambda a: (a & (seqs - 1)) * steps + (a >> seqs.bit_length() - 1))
    x[m] = matmul(order, tokens_ref[...]).astype(jnp.bfloat16)
    for d in (2, 1, 0):
        input_copy(d, m).start()

    lanes = 128
    per_row = lanes // 4
    odd = q // per_row
    row = lax.broadcasted_iota(jnp.int32, (lanes, lanes), 0)
    col = lax.broadcasted_iota(jnp.int32, (lanes, lanes), 1)
    mine = ((col >> 2) == q % per_row) & ((row & 1) == odd)
    entries = jnp.where(mine, table_ref[...] - q * 256, 0).astype(jnp.float32).astype(jnp.bfloat16)
    spread = matmul(one_hot(256, lanes, lambda a: (a >> 2) * 2 + odd), entries)
    row = lax.broadcasted_iota(jnp.int32, (256, lanes), 0)
    col = lax.broadcasted_iota(jnp.int32, (256, lanes), 1)
    wanted = col == (q % per_row) * 4 + (row & 3)
    picked = jnp.sum(jnp.where(wanted, spread, 0.0), axis=1, keepdims=True)
    channel = lax.broadcasted_iota(jnp.int32, (256, 256), 1).astype(jnp.float32)
    pt[...] = jnp.where(channel == picked, 1.0, 0.0).astype(jnp.bfloat16)

    def rows_of(arr, i):
        return w.at[arr, pl.ds(i * 16, 16)]

    @pl.loop(0, ITEMS)
    def _(n):
        tick(n)

    for d in range(3):
        input_copy(d, mates[d]).wait_recv()
        input_copy(d, m).wait_send()

    @pl.loop(0, 4)
    def _(c):
        cols = pl.ds(pl.multiple_of(c * 256, 256), 256)
        total = bias_ref[0:1, cols]
        for i in range(SPLIT):
            total = total + matmul(x[i], w[0, pl.ds(i * 16, 16), :, cols].reshape(256, 256))
        proj[:, :, :, cols] = total.reshape(steps, PARTS, part, 256)
        tick(ITEMS + c)

    def update(gate, states, layer, t, h, first=False):
        ingate = sigmoid(gate(0))
        cellgate = jnp.tanh(gate(2))
        now = ingate * cellgate
        if not first:
            now = now + sigmoid(gate(1)) * cell[h]
        outgate = sigmoid(gate(3))
        cell[h] = now
        states[t, h, m] = (outgate * jnp.tanh(now)).astype(jnp.bfloat16)

    def send_state(states, layer, t, h):
        for d in (1, 2, 0):
            state_copy(states, layer, t, h, d, m).start()

    def start(states, layer):
        for h in range(PARTS):
            update(lambda k: proj[0, h, :, k * 256 : k * 256 + 256], states, layer, 0, h, first=True)
            send_state(states, layer, 0, h)

    def step(states, layer, t, h):
        arr = 2 * layer + 1

        state_copy(states, layer, t - 1, h, 0, mates[0]).wait_recv()
        near = jnp.concatenate([states[t - 1, h, here + i] for i in range(2)], axis=1)
        pre = proj[t, h] + matmul(near, w[arr, pl.ds(here * 16, 32)].reshape(512, 1024))
        for d in (1, 2):
            state_copy(states, layer, t - 1, h, d, mates[d]).wait_recv()
            far = states[t - 1, h, mates[d]]
            pre = pre + matmul(far, w[arr, pl.ds(mates[d] * 16, 16)].reshape(256, 1024))
        update(lambda k: pre[:, k * 256 : k * 256 + 256], states, layer, t, h)

        @pl.when(t < steps - 1)
        def _():
            send_state(states, layer, t, h)

        for d in range(3):
            state_copy(states, layer, t - 1, h, d, m).wait_send()

    def forward(p):
        shuffled_all(p).wait_recv()
        for d in range(3):
            mixed_copy(p, d, m).start()

    start(s0, 0)

    @pl.loop(ITEMS + 4, 2 * ITEMS)
    def _(n):
        tick(n)

    @pl.loop(1, steps)
    def _(t):
        p = t // 2
        n = 2 * ITEMS + 3 * (t - 1)
        step(s0, 0, t, 0)
        tick(n)
        for h in range(1, PARTS):
            step(s0, 0, t, h)
        tick(n + 1)

        @pl.when(t % 2 == 1)
        def _():
            pair = jnp.concatenate([s0[t - 1 + h // PARTS, h % PARTS, m] for h in range(2 * PARTS)], axis=0)
            moved = lax.dot_general(
                pt[...], pair, (((1,), (1,)), ((), ())), preferred_element_type=jnp.float32
            )
            obuf[p] = moved.astype(jnp.bfloat16).reshape(groups, 16, 128)
            r[p, m, g] = obuf[p, g]

            @pl.loop(1, groups)
            def _(d):
                other = (g + d) % groups
                pltpu.make_async_remote_copy(
                    src_ref=obuf.at[p, other], dst_ref=r.at[p, m, g],
                    send_sem=osend.at[p], recv_sem=orecv.at[p],
                    device_id=(other * SPLIT + m, z), device_id_type=MESH,
                ).start()

        @pl.when(t % 2 == 0)
        def _():
            forward(p - 1)

        tick(n + 2)

    swap = one_hot(64, 64, lambda a: ((a >> 2) & 3) * 16 + (a >> 4) * 4 + (a & 3))

    @pl.loop(0, groups)
    def _(i):
        block = jnp.concatenate([w[2, j * 16 + i] for j in range(SPLIT)], axis=0)
        block = matmul(swap, block).astype(jnp.bfloat16).reshape(SPLIT, 16, 1024)
        for j in range(SPLIT):
            wperm[j * 16 + i] = block[j]

        @pl.when(i % 8 == 7)
        def _():
            tick(4 * ITEMS - 7 + i // 8)

    tick(4 * ITEMS - 5)
    forward(steps // 2 - 1)

    def project_mixed(p):
        shuffled_all(p).wait_send()
        for d in range(3):
            mixed_copy(p, d, mates[d]).wait_recv()
            mixed_copy(p, d, m).wait_send()
        total = lax.dot_general(
            r[p].reshape(1024, 128), wperm[...].reshape(1024, 1024),
            (((0,), (0,)), ((), ())), preferred_element_type=jnp.float32,
        )
        proj[pl.ds(2 * p, 2)] = (total + bias_ref[1:2, :]).reshape(2, PARTS, part, 1024)

    @pl.loop(0, steps // 2 - 1)
    def _(p):
        project_mixed(p)

    def stored(t):
        return pltpu.make_async_copy(s1.at[t, 0, m], out_ref.at[t], done.at[t])

    def store(t):
        stored(t).start()

    start(s1, 1)

    for n in range(4 * ITEMS - DEPTH, 4 * ITEMS):
        tick(n, False)

    @pl.loop(1, steps)
    def _(t):
        for h in range(PARTS):
            step(s1, 1, t, h)
        store(t - 1)

        @pl.when(t == 1)
        def _():
            project_mixed(steps // 2 - 1)

    store(steps - 1)

    @pl.loop(0, steps)
    def _(t):
        stored(t).wait()


def local(tokens, input_weights, recur_weights, biases, shuffle):
    seqs, steps, units = tokens.shape
    depth = input_weights.shape[1]
    bf16 = jnp.bfloat16
    hbm = pl.BlockSpec(memory_space=pl.ANY)
    dma = pltpu.SemaphoreType.DMA
    pairs = steps // 2
    out = pl.pallas_call(
        kernel,
        out_shape=jax.ShapeDtypeStruct((steps, seqs, units), bf16),
        in_specs=[hbm] * 5,
        out_specs=hbm,
        scratch_shapes=[
            pltpu.VMEM((seqs * steps, units), bf16),
            pltpu.VMEM((2, 1024), jnp.float32),
            pltpu.VMEM((128, 128), jnp.int32),
            pltpu.VMEM((4, 64, 16, 1024), bf16),
            pltpu.VMEM((64, 16, 1024), bf16),
            pltpu.VMEM((SPLIT, seqs * steps, units), bf16),
            pltpu.VMEM((steps, PARTS, seqs // PARTS, 1024), jnp.float32),
            pltpu.VMEM((steps, PARTS, SPLIT, seqs // PARTS, units), bf16),
            pltpu.VMEM((steps, PARTS, SPLIT, seqs // PARTS, units), bf16),
            pltpu.VMEM((pairs, 16, 16, 128), bf16),
            pltpu.VMEM((pairs, SPLIT, 16, 16, 128), bf16),
            pltpu.VMEM((PARTS, seqs // PARTS, units), jnp.float32),
            pltpu.VMEM((256, 256), bf16),
            dma((7,)),
            dma((4 * ITEMS, 2)),
            dma((4 * ITEMS, 2)),
            dma((3,)),
            dma((3,)),
            dma((2, steps, PARTS, 3)),
            dma((2, steps, PARTS, 3)),
            dma((pairs,)),
            dma((pairs,)),
            dma((pairs, 3)),
            dma((pairs, 3)),
            dma((steps,)),
        ],
        compiler_params=pltpu.CompilerParams(
            collective_id=0, has_side_effects=True, vmem_limit_bytes=63 * 1024 * 1024
        ),
    )(
        tokens.reshape(seqs * steps, units),
        input_weights.reshape(2, depth // 16, 16, 1024),
        recur_weights.reshape(2, depth // 16, 16, 1024),
        biases,
        shuffle.reshape(128, 128),
    )
    return jnp.transpose(out, (1, 0, 2))


def solution(mesh):
    return jax.shard_map(
        local,
        mesh=mesh,
        in_specs=(
            P("batch", None, "grp"),
            P(None, "batch", "grp"),
            P(None, "batch", "grp"),
            P(None, "grp"),
            P(),
        ),
        out_specs=P("batch", None, "grp"),
        check_vma=False,
    )
```

```python
import jax
import jax.numpy as jnp
from jax import lax
from jax.experimental import pallas as pl
from jax.experimental.pallas import tpu as pltpu
from jax.sharding import PartitionSpec as P

MESH = pl.DeviceIdType.MESH
DEPTH = 4
SPLIT = 4
PARTS = 1
ITEMS = 14


def one_hot(rows, cols, target):
    row = lax.broadcasted_iota(jnp.int32, (rows, cols), 0)
    col = lax.broadcasted_iota(jnp.int32, (rows, cols), 1)
    return (col == target(row)).astype(jnp.float32).astype(jnp.bfloat16)


def sigmoid(x):
    return 0.5 * jnp.tanh(0.5 * x) + 0.5


def matmul(a, b):
    return jnp.dot(a, b, preferred_element_type=jnp.float32)


def kernel(
    tokens_hbm, win_ref, wrec_ref, bias_hbm, table_hbm, out_ref,
    tokens_ref, bias_ref, table_ref, w, wperm, x, proj, s0, s1, obuf, r, cell, pt,
    local_sem, wsend, wrecv, xsend, xrecv, ssend, srecv, osend, orecv, gsend, grecv, done,
):
    groups = lax.axis_size("grp") // SPLIT
    ring = lax.axis_size("batch")
    q = lax.axis_index("grp")
    z = lax.axis_index("batch")
    g = q // SPLIT
    m = q % SPLIT
    mates = (m + 1 - 2 * (m % 2), (m + 2) % SPLIT, SPLIT - 1 - m)

    here = m // 2 * 2

    def mate(d):
        return (g * SPLIT + mates[d], z)

    up = (q, (z + 1) % ring)
    down = (q, (z + ring - 1) % ring)

    loads = []
    for layer in range(2):
        for kind, ref in enumerate((win_ref, wrec_ref)):
            arr = 2 * layer + kind
            load = pltpu.make_async_copy(
                ref.at[layer], w.at[arr, pl.ds(z * 8, 8)], local_sem.at[arr]
            )
            load.start()
            loads.append(load)

    small = []
    for n, (ref, copy) in enumerate(
        ((tokens_hbm, tokens_ref), (bias_hbm, bias_ref), (table_hbm, table_ref))
    ):
        load = pltpu.make_async_copy(ref, copy, local_sem.at[4 + n])
        load.start()
        small.append(load)

    barrier = pltpu.get_barrier_semaphore()
    for device in (up, down, mate(0), mate(1), mate(2)):
        pl.semaphore_signal(barrier, inc=1, device_id=device, device_id_type=MESH)

    @pl.loop(1, groups)
    def _(d):
        other = (g + d) % groups
        pl.semaphore_signal(
            barrier, inc=1, device_id=(other * SPLIT + m, z), device_id_type=MESH
        )

    def item(n, way, came):
        arr, j = n // ITEMS, n % ITEMS
        hop, piece = j // DEPTH, j % DEPTH
        if way == 0:
            origin = (z + 2 * ring - hop - came) % ring
            device = up
        else:
            piece = (piece + DEPTH // 2) % DEPTH
            origin = (z + hop + came) % ring
            device = down
        view = w.at[arr, pl.ds(origin * 8 + piece * 2, 2)]
        return pltpu.make_async_remote_copy(
            src_ref=view, dst_ref=view, send_sem=wsend.at[n, way], recv_sem=wrecv.at[n, way],
            device_id=device, device_id_type=MESH,
        )

    def tick(n, more=True):
        for way in range(2):
            item(n, way, 1).wait_recv()
            if more:
                item(n + DEPTH, way, 0).start()
            item(n, way, 0).wait_send()

    def state_copy(states, layer, t, h, d, owner):
        view = states.at[t, h, owner]
        return pltpu.make_async_remote_copy(
            src_ref=view, dst_ref=view,
            send_sem=ssend.at[layer, t, h, d], recv_sem=srecv.at[layer, t, h, d],
            device_id=mate(d), device_id_type=MESH,
        )

    def input_copy(d, owner):
        view = x.at[owner]
        return pltpu.make_async_remote_copy(
            src_ref=view, dst_ref=view, send_sem=xsend.at[d], recv_sem=xrecv.at[d],
            device_id=mate(d), device_id_type=MESH,
        )

    def mixed_copy(p, d, owner):
        view = r.at[p, owner]
        return pltpu.make_async_remote_copy(
            src_ref=view, dst_ref=view, send_sem=gsend.at[p, d], recv_sem=grecv.at[p, d],
            device_id=mate(d), device_id_type=MESH,
        )

    def shuffled_all(p):
        return pltpu.make_async_remote_copy(
            src_ref=obuf.at[p, pl.ds(0, groups - 1)], dst_ref=r.at[p, m, pl.ds(0, groups - 1)],
            send_sem=osend.at[p], recv_sem=orecv.at[p], device_id=mate(0), device_id_type=MESH,
        )

    loads[0].wait()
    pl.semaphore_wait(barrier, 5 + groups - 1)
    for n in range(DEPTH):
        for way in range(2):
            item(n, way, 0).start()

    for load in small + loads[1:]:
        load.wait()

    rows = tokens_ref.shape[0]
    steps = proj.shape[0]
    seqs = rows // steps
    part = seqs // PARTS
    order = one_hot(rows, rows, lambda a: (a & (seqs - 1)) * steps + (a >> seqs.bit_length() - 1))
    x[m] = matmul(order, tokens_ref[...]).astype(jnp.bfloat16)
    for d in (2, 1, 0):
        input_copy(d, m).start()

    lanes = 128
    per_row = lanes // 4
    odd = q // per_row
    row = lax.broadcasted_iota(jnp.int32, (lanes, lanes), 0)
    col = lax.broadcasted_iota(jnp.int32, (lanes, lanes), 1)
    mine = ((col >> 2) == q % per_row) & ((row & 1) == odd)
    entries = jnp.where(mine, table_ref[...] - q * 256, 0).astype(jnp.float32).astype(jnp.bfloat16)
    spread = matmul(one_hot(256, lanes, lambda a: (a >> 2) * 2 + odd), entries)
    row = lax.broadcasted_iota(jnp.int32, (256, lanes), 0)
    col = lax.broadcasted_iota(jnp.int32, (256, lanes), 1)
    wanted = col == (q % per_row) * 4 + (row & 3)
    picked = jnp.sum(jnp.where(wanted, spread, 0.0), axis=1, keepdims=True)
    channel = lax.broadcasted_iota(jnp.int32, (256, 256), 1).astype(jnp.float32)
    pt[...] = jnp.where(channel == picked, 1.0, 0.0).astype(jnp.bfloat16)

    def rows_of(arr, i):
        return w.at[arr, pl.ds(i * 16, 16)]

    @pl.loop(0, ITEMS)
    def _(n):
        tick(n)

    for d in range(3):
        input_copy(d, mates[d]).wait_recv()
        input_copy(d, m).wait_send()

    @pl.loop(0, 4)
    def _(c):
        cols = pl.ds(pl.multiple_of(c * 256, 256), 256)
        total = bias_ref[0:1, cols]
        for i in range(SPLIT):
            total = total + matmul(x[i], w[0, pl.ds(i * 16, 16), :, cols].reshape(256, 256))
        proj[:, :, :, cols] = total.reshape(steps, PARTS, part, 256)
        tick(ITEMS + c)

    def update(gate, states, layer, t, h, first=False):
        ingate = sigmoid(gate(0))
        cellgate = jnp.tanh(gate(2))
        now = ingate * cellgate
        if not first:
            now = now + sigmoid(gate(1)) * cell[h]
        outgate = sigmoid(gate(3))
        cell[h] = now
        states[t, h, m] = (outgate * jnp.tanh(now)).astype(jnp.bfloat16)

    def send_state(states, layer, t, h):
        for d in (1, 2, 0):
            state_copy(states, layer, t, h, d, m).start()

    def start(states, layer):
        for h in range(PARTS):
            update(lambda k: proj[0, h, :, k * 256 : k * 256 + 256], states, layer, 0, h, first=True)
            send_state(states, layer, 0, h)

    def step(states, layer, t, h):
        arr = 2 * layer + 1

        state_copy(states, layer, t - 1, h, 0, mates[0]).wait_recv()
        near = jnp.concatenate([states[t - 1, h, here + i] for i in range(2)], axis=1)
        pre = proj[t, h] + matmul(near, w[arr, pl.ds(here * 16, 32)].reshape(512, 1024))
        for d in (1, 2):
            state_copy(states, layer, t - 1, h, d, mates[d]).wait_recv()
            far = states[t - 1, h, mates[d]]
            pre = pre + matmul(far, w[arr, pl.ds(mates[d] * 16, 16)].reshape(256, 1024))
        update(lambda k: pre[:, k * 256 : k * 256 + 256], states, layer, t, h)

        @pl.when(t < steps - 1)
        def _():
            send_state(states, layer, t, h)

        for d in range(3):
            state_copy(states, layer, t - 1, h, d, m).wait_send()

    def forward(p):
        shuffled_all(p).wait_recv()
        for d in range(3):
            mixed_copy(p, d, m).start()

    start(s0, 0)

    @pl.loop(ITEMS + 4, 2 * ITEMS)
    def _(n):
        tick(n)

    @pl.loop(1, steps)
    def _(t):
        p = t // 2
        n = 2 * ITEMS + 3 * (t - 1)
        step(s0, 0, t, 0)
        tick(n)
        for h in range(1, PARTS):
            step(s0, 0, t, h)
        tick(n + 1)

        @pl.when(t % 2 == 1)
        def _():
            pair = jnp.concatenate([s0[t - 1 + h // PARTS, h % PARTS, m] for h in range(2 * PARTS)], axis=0)
            moved = lax.dot_general(
                pt[...], pair, (((1,), (1,)), ((), ())), preferred_element_type=jnp.float32
            )
            obuf[p] = moved.astype(jnp.bfloat16).reshape(groups, 16, 128)
            r[p, m, g] = obuf[p, g]

            @pl.loop(1, groups)
            def _(d):
                other = (g + d) % groups
                pltpu.make_async_remote_copy(
                    src_ref=obuf.at[p, other], dst_ref=r.at[p, m, g],
                    send_sem=osend.at[p], recv_sem=orecv.at[p],
                    device_id=(other * SPLIT + m, z), device_id_type=MESH,
                ).start()

        @pl.when(t % 2 == 0)
        def _():
            forward(p - 1)

        tick(n + 2)

    swap = one_hot(
        256, 256, lambda a: (a & 192) + ((a >> 2) & 3) * 16 + ((a >> 4) & 3) * 4 + (a & 3)
    )

    @pl.loop(0, groups // 4)
    def _(v):
        block = jnp.concatenate(
            [w[2, j * 16 + 4 * v + i] for i in range(4) for j in range(SPLIT)], axis=0
        )
        block = matmul(swap, block).astype(jnp.bfloat16).reshape(4, SPLIT, 16, 1024)
        for i in range(4):
            for j in range(SPLIT):
                wperm[j * 16 + 4 * v + i] = block[i, j]

        @pl.when(v % 2 == 1)
        def _():
            tick(4 * ITEMS - 7 + v // 2)

    tick(4 * ITEMS - 5)

    def project_mixed(p):
        shuffled_all(p).wait_send()
        for d in range(3):
            mixed_copy(p, d, mates[d]).wait_recv()
            mixed_copy(p, d, m).wait_send()
        total = lax.dot_general(
            r[p].reshape(1024, 128), wperm[...].reshape(1024, 1024),
            (((0,), (0,)), ((), ())), preferred_element_type=jnp.float32,
        )
        proj[pl.ds(2 * p, 2)] = (total + bias_ref[1:2, :]).reshape(2, PARTS, part, 1024)

    project_mixed(0)

    def stored(t):
        return pltpu.make_async_copy(s1.at[t, 0, m], out_ref.at[t], done.at[t])

    def store(t):
        stored(t).start()

    start(s1, 1)
    forward(steps // 2 - 1)

    @pl.loop(1, steps // 2 - 1)
    def _(p):
        project_mixed(p)

    for n in range(4 * ITEMS - DEPTH, 4 * ITEMS):
        tick(n, False)

    @pl.loop(1, steps)
    def _(t):
        for h in range(PARTS):
            step(s1, 1, t, h)
        store(t - 1)

        @pl.when(t == 1)
        def _():
            project_mixed(steps // 2 - 1)

    store(steps - 1)

    @pl.loop(0, steps)
    def _(t):
        stored(t).wait()


def local(tokens, input_weights, recur_weights, biases, shuffle):
    seqs, steps, units = tokens.shape
    depth = input_weights.shape[1]
    bf16 = jnp.bfloat16
    hbm = pl.BlockSpec(memory_space=pl.ANY)
    dma = pltpu.SemaphoreType.DMA
    pairs = steps // 2
    out = pl.pallas_call(
        kernel,
        out_shape=jax.ShapeDtypeStruct((steps, seqs, units), bf16),
        in_specs=[hbm] * 5,
        out_specs=hbm,
        scratch_shapes=[
            pltpu.VMEM((seqs * steps, units), bf16),
            pltpu.VMEM((2, 1024), jnp.float32),
            pltpu.VMEM((128, 128), jnp.int32),
            pltpu.VMEM((4, 64, 16, 1024), bf16),
            pltpu.VMEM((64, 16, 1024), bf16),
            pltpu.VMEM((SPLIT, seqs * steps, units), bf16),
            pltpu.VMEM((steps, PARTS, seqs // PARTS, 1024), jnp.float32),
            pltpu.VMEM((steps, PARTS, SPLIT, seqs // PARTS, units), bf16),
            pltpu.VMEM((steps, PARTS, SPLIT, seqs // PARTS, units), bf16),
            pltpu.VMEM((pairs, 16, 16, 128), bf16),
            pltpu.VMEM((pairs, SPLIT, 16, 16, 128), bf16),
            pltpu.VMEM((PARTS, seqs // PARTS, units), jnp.float32),
            pltpu.VMEM((256, 256), bf16),
            dma((7,)),
            dma((4 * ITEMS, 2)),
            dma((4 * ITEMS, 2)),
            dma((3,)),
            dma((3,)),
            dma((2, steps, PARTS, 3)),
            dma((2, steps, PARTS, 3)),
            dma((pairs,)),
            dma((pairs,)),
            dma((pairs, 3)),
            dma((pairs, 3)),
            dma((steps,)),
        ],
        compiler_params=pltpu.CompilerParams(
            collective_id=0, has_side_effects=True, vmem_limit_bytes=63 * 1024 * 1024
        ),
    )(
        tokens.reshape(seqs * steps, units),
        input_weights.reshape(2, depth // 16, 16, 1024),
        recur_weights.reshape(2, depth // 16, 16, 1024),
        biases,
        shuffle.reshape(128, 128),
    )
    return jnp.transpose(out, (1, 0, 2))


def solution(mesh):
    return jax.shard_map(
        local,
        mesh=mesh,
        in_specs=(
            P("batch", None, "grp"),
            P(None, "batch", "grp"),
            P(None, "batch", "grp"),
            P(None, "grp"),
            P(),
        ),
        out_specs=P("batch", None, "grp"),
        check_vma=False,
    )
```

```python
import jax
import jax.numpy as jnp
from jax import lax
from jax.experimental import pallas as pl
from jax.experimental.pallas import tpu as pltpu
from jax.sharding import PartitionSpec as P

MESH = pl.DeviceIdType.MESH
DEPTH = 4
SPLIT = 4
PARTS = 1
ITEMS = 14


def one_hot(rows, cols, target):
    row = lax.broadcasted_iota(jnp.int32, (rows, cols), 0)
    col = lax.broadcasted_iota(jnp.int32, (rows, cols), 1)
    return (col == target(row)).astype(jnp.float32).astype(jnp.bfloat16)


def sigmoid(x):
    return 0.5 * jnp.tanh(0.5 * x) + 0.5


def matmul(a, b):
    return jnp.dot(a, b, preferred_element_type=jnp.float32)


def kernel(
    tokens_hbm, win_ref, wrec_ref, bias_hbm, table_hbm, out_ref,
    tokens_ref, bias_ref, table_ref, w, wperm, x, proj, s0, s1, obuf, r, cell, pt,
    local_sem, wsend, wrecv, xsend, xrecv, ssend, srecv, osend, orecv, gsend, grecv, done,
):
    groups = lax.axis_size("grp") // SPLIT
    ring = lax.axis_size("batch")
    q = lax.axis_index("grp")
    z = lax.axis_index("batch")
    g = q // SPLIT
    m = q % SPLIT
    mates = (m + 1 - 2 * (m % 2), (m + 2) % SPLIT, SPLIT - 1 - m)

    here = m // 2 * 2

    def mate(d):
        return (g * SPLIT + mates[d], z)

    up = (q, (z + 1) % ring)
    down = (q, (z + ring - 1) % ring)

    loads = []
    for layer in range(2):
        for kind, ref in enumerate((win_ref, wrec_ref)):
            arr = 2 * layer + kind
            load = pltpu.make_async_copy(
                ref.at[layer], w.at[arr, pl.ds(z * 8, 8)], local_sem.at[arr]
            )
            load.start()
            loads.append(load)

    small = []
    for n, (ref, copy) in enumerate(
        ((tokens_hbm, tokens_ref), (bias_hbm, bias_ref), (table_hbm, table_ref))
    ):
        load = pltpu.make_async_copy(ref, copy, local_sem.at[4 + n])
        load.start()
        small.append(load)

    barrier = pltpu.get_barrier_semaphore()
    for device in (up, down, mate(0), mate(1), mate(2)):
        pl.semaphore_signal(barrier, inc=1, device_id=device, device_id_type=MESH)

    @pl.loop(1, groups)
    def _(d):
        other = (g + d) % groups
        pl.semaphore_signal(
            barrier, inc=1, device_id=(other * SPLIT + m, z), device_id_type=MESH
        )

    def item(n, way, came):
        arr, j = n // ITEMS, n % ITEMS
        hop, piece = j // DEPTH, j % DEPTH
        if way == 0:
            origin = (z + 2 * ring - hop - came) % ring
            device = up
        else:
            piece = (piece + DEPTH // 2) % DEPTH
            origin = (z + hop + came) % ring
            device = down
        view = w.at[arr, pl.ds(origin * 8 + piece * 2, 2)]
        return pltpu.make_async_remote_copy(
            src_ref=view, dst_ref=view, send_sem=wsend.at[n, way], recv_sem=wrecv.at[n, way],
            device_id=device, device_id_type=MESH,
        )

    def tick(n, more=True):
        for way in range(2):
            item(n, way, 1).wait_recv()
            if more:
                item(n + DEPTH, way, 0).start()
            item(n, way, 0).wait_send()

    def state_copy(states, layer, t, h, d, owner):
        view = states.at[t, h, owner]
        return pltpu.make_async_remote_copy(
            src_ref=view, dst_ref=view,
            send_sem=ssend.at[layer, t, h, d], recv_sem=srecv.at[layer, t, h, d],
            device_id=mate(d), device_id_type=MESH,
        )

    def input_copy(d, owner):
        view = x.at[owner]
        return pltpu.make_async_remote_copy(
            src_ref=view, dst_ref=view, send_sem=xsend.at[d], recv_sem=xrecv.at[d],
            device_id=mate(d), device_id_type=MESH,
        )

    def mixed_copy(p, d, owner):
        view = r.at[p, owner]
        return pltpu.make_async_remote_copy(
            src_ref=view, dst_ref=view, send_sem=gsend.at[p, d], recv_sem=grecv.at[p, d],
            device_id=mate(d), device_id_type=MESH,
        )

    def shuffled_all(p):
        return pltpu.make_async_remote_copy(
            src_ref=obuf.at[p, pl.ds(0, groups - 1)], dst_ref=r.at[p, m, pl.ds(0, groups - 1)],
            send_sem=osend.at[p], recv_sem=orecv.at[p], device_id=mate(0), device_id_type=MESH,
        )

    loads[0].wait()
    pl.semaphore_wait(barrier, 5 + groups - 1)
    for n in range(DEPTH):
        for way in range(2):
            item(n, way, 0).start()

    for load in small + loads[1:]:
        load.wait()

    rows = tokens_ref.shape[0]
    steps = proj.shape[0]
    seqs = rows // steps
    part = seqs // PARTS
    order = one_hot(rows, rows, lambda a: (a & (seqs - 1)) * steps + (a >> seqs.bit_length() - 1))
    x[m] = matmul(order, tokens_ref[...]).astype(jnp.bfloat16)
    for d in (2, 1, 0):
        input_copy(d, m).start()
    for n in range(2):
        tick(n)

    lanes = 128
    per_row = lanes // 4
    odd = q // per_row
    row = lax.broadcasted_iota(jnp.int32, (lanes, lanes), 0)
    col = lax.broadcasted_iota(jnp.int32, (lanes, lanes), 1)
    mine = ((col >> 2) == q % per_row) & ((row & 1) == odd)
    entries = jnp.where(mine, table_ref[...] - q * 256, 0).astype(jnp.float32).astype(jnp.bfloat16)
    spread = matmul(one_hot(256, lanes, lambda a: (a >> 2) * 2 + odd), entries)
    row = lax.broadcasted_iota(jnp.int32, (256, lanes), 0)
    col = lax.broadcasted_iota(jnp.int32, (256, lanes), 1)
    wanted = col == (q % per_row) * 4 + (row & 3)
    picked = jnp.sum(jnp.where(wanted, spread, 0.0), axis=1, keepdims=True)
    channel = lax.broadcasted_iota(jnp.int32, (256, 256), 1).astype(jnp.float32)
    pt[...] = jnp.where(channel == picked, 1.0, 0.0).astype(jnp.bfloat16)

    def rows_of(arr, i):
        return w.at[arr, pl.ds(i * 16, 16)]

    @pl.loop(2, ITEMS)
    def _(n):
        tick(n)

    for d in range(3):
        input_copy(d, mates[d]).wait_recv()
        input_copy(d, m).wait_send()

    @pl.loop(0, 4)
    def _(c):
        cols = pl.ds(pl.multiple_of(c * 256, 256), 256)
        total = bias_ref[0:1, cols]
        for i in range(SPLIT):
            total = total + matmul(x[i], w[0, pl.ds(i * 16, 16), :, cols].reshape(256, 256))
        proj[:, :, :, cols] = total.reshape(steps, PARTS, part, 256)
        tick(ITEMS + c)

    def update(gate, states, layer, t, h, first=False):
        ingate = sigmoid(gate(0))
        cellgate = jnp.tanh(gate(2))
        now = ingate * cellgate
        if not first:
            now = now + sigmoid(gate(1)) * cell[h]
        outgate = sigmoid(gate(3))
        cell[h] = now
        states[t, h, m] = (outgate * jnp.tanh(now)).astype(jnp.bfloat16)

    def send_state(states, layer, t, h):
        for d in (1, 2, 0):
            state_copy(states, layer, t, h, d, m).start()

    def start(states, layer):
        for h in range(PARTS):
            update(lambda k: proj[0, h, :, k * 256 : k * 256 + 256], states, layer, 0, h, first=True)
            send_state(states, layer, 0, h)

    def step(states, layer, t, h, between=None):
        arr = 2 * layer + 1

        state_copy(states, layer, t - 1, h, 0, mates[0]).wait_recv()
        near = jnp.concatenate([states[t - 1, h, here + i] for i in range(2)], axis=1)
        pre = proj[t, h] + matmul(near, w[arr, pl.ds(here * 16, 32)].reshape(512, 1024))
        if between is not None:
            between()
        for d in (1, 2):
            state_copy(states, layer, t - 1, h, d, mates[d]).wait_recv()
            far = states[t - 1, h, mates[d]]
            pre = pre + matmul(far, w[arr, pl.ds(mates[d] * 16, 16)].reshape(256, 1024))
        update(lambda k: pre[:, k * 256 : k * 256 + 256], states, layer, t, h)

        @pl.when(t < steps - 1)
        def _():
            send_state(states, layer, t, h)

        for d in range(3):
            state_copy(states, layer, t - 1, h, d, m).wait_send()

    def forward(p):
        shuffled_all(p).wait_recv()
        for d in range(3):
            mixed_copy(p, d, m).start()

    start(s0, 0)

    @pl.loop(ITEMS + 4, 2 * ITEMS)
    def _(n):
        tick(n)

    @pl.loop(1, steps)
    def _(t):
        p = t // 2
        n = 2 * ITEMS + 3 * (t - 1)
        step(s0, 0, t, 0, between=lambda: tick(n))
        for h in range(1, PARTS):
            step(s0, 0, t, h)
        tick(n + 1)

        @pl.when(t % 2 == 1)
        def _():
            pair = jnp.concatenate([s0[t - 1 + h // PARTS, h % PARTS, m] for h in range(2 * PARTS)], axis=0)
            moved = lax.dot_general(
                pt[...], pair, (((1,), (1,)), ((), ())), preferred_element_type=jnp.float32
            )
            obuf[p] = moved.astype(jnp.bfloat16).reshape(groups, 16, 128)
            r[p, m, g] = obuf[p, g]

            @pl.loop(1, groups)
            def _(d):
                other = (g + d) % groups
                pltpu.make_async_remote_copy(
                    src_ref=obuf.at[p, other], dst_ref=r.at[p, m, g],
                    send_sem=osend.at[p], recv_sem=orecv.at[p],
                    device_id=(other * SPLIT + m, z), device_id_type=MESH,
                ).start()

        @pl.when(t % 2 == 0)
        def _():
            forward(p - 1)

        tick(n + 2)

    swap = one_hot(
        256, 256, lambda a: (a & 192) + ((a >> 2) & 3) * 16 + ((a >> 4) & 3) * 4 + (a & 3)
    )

    @pl.loop(0, groups // 4)
    def _(v):
        block = jnp.concatenate(
            [w[2, j * 16 + 4 * v + i] for i in range(4) for j in range(SPLIT)], axis=0
        )
        block = matmul(swap, block).astype(jnp.bfloat16).reshape(4, SPLIT, 16, 1024)
        for i in range(4):
            for j in range(SPLIT):
                wperm[j * 16 + 4 * v + i] = block[i, j]

        @pl.when(v % 2 == 1)
        def _():
            tick(4 * ITEMS - 7 + v // 2)

    tick(4 * ITEMS - 5)

    def project_mixed(p):
        shuffled_all(p).wait_send()
        for d in range(3):
            mixed_copy(p, d, mates[d]).wait_recv()
            mixed_copy(p, d, m).wait_send()
        total = lax.dot_general(
            r[p].reshape(1024, 128), wperm[...].reshape(1024, 1024),
            (((0,), (0,)), ((), ())), preferred_element_type=jnp.float32,
        )
        proj[pl.ds(2 * p, 2)] = (total + bias_ref[1:2, :]).reshape(2, PARTS, part, 1024)

    project_mixed(0)

    def stored(t):
        return pltpu.make_async_copy(s1.at[t, 0, m], out_ref.at[t], done.at[t])

    def store(t):
        stored(t).start()

    start(s1, 1)
    forward(steps // 2 - 1)

    @pl.loop(1, steps // 2 - 1)
    def _(p):
        project_mixed(p)

    for n in range(4 * ITEMS - DEPTH, 4 * ITEMS):
        tick(n, False)

    @pl.loop(1, steps)
    def _(t):
        for h in range(PARTS):
            step(s1, 1, t, h)
        store(t - 1)

        @pl.when(t == 1)
        def _():
            project_mixed(steps // 2 - 1)

    store(steps - 1)

    @pl.loop(0, steps)
    def _(t):
        stored(t).wait()


def local(tokens, input_weights, recur_weights, biases, shuffle):
    seqs, steps, units = tokens.shape
    depth = input_weights.shape[1]
    bf16 = jnp.bfloat16
    hbm = pl.BlockSpec(memory_space=pl.ANY)
    dma = pltpu.SemaphoreType.DMA
    pairs = steps // 2
    out = pl.pallas_call(
        kernel,
        out_shape=jax.ShapeDtypeStruct((steps, seqs, units), bf16),
        in_specs=[hbm] * 5,
        out_specs=hbm,
        scratch_shapes=[
            pltpu.VMEM((seqs * steps, units), bf16),
            pltpu.VMEM((2, 1024), jnp.float32),
            pltpu.VMEM((128, 128), jnp.int32),
            pltpu.VMEM((4, 64, 16, 1024), bf16),
            pltpu.VMEM((64, 16, 1024), bf16),
            pltpu.VMEM((SPLIT, seqs * steps, units), bf16),
            pltpu.VMEM((steps, PARTS, seqs // PARTS, 1024), jnp.float32),
            pltpu.VMEM((steps, PARTS, SPLIT, seqs // PARTS, units), bf16),
            pltpu.VMEM((steps, PARTS, SPLIT, seqs // PARTS, units), bf16),
            pltpu.VMEM((pairs, 16, 16, 128), bf16),
            pltpu.VMEM((pairs, SPLIT, 16, 16, 128), bf16),
            pltpu.VMEM((PARTS, seqs // PARTS, units), jnp.float32),
            pltpu.VMEM((256, 256), bf16),
            dma((7,)),
            dma((4 * ITEMS, 2)),
            dma((4 * ITEMS, 2)),
            dma((3,)),
            dma((3,)),
            dma((2, steps, PARTS, 3)),
            dma((2, steps, PARTS, 3)),
            dma((pairs,)),
            dma((pairs,)),
            dma((pairs, 3)),
            dma((pairs, 3)),
            dma((steps,)),
        ],
        compiler_params=pltpu.CompilerParams(
            collective_id=0, has_side_effects=True, vmem_limit_bytes=63 * 1024 * 1024
        ),
    )(
        tokens.reshape(seqs * steps, units),
        input_weights.reshape(2, depth // 16, 16, 1024),
        recur_weights.reshape(2, depth // 16, 16, 1024),
        biases,
        shuffle.reshape(128, 128),
    )
    return jnp.transpose(out, (1, 0, 2))


def solution(mesh):
    return jax.shard_map(
        local,
        mesh=mesh,
        in_specs=(
            P("batch", None, "grp"),
            P(None, "batch", "grp"),
            P(None, "batch", "grp"),
            P(None, "grp"),
            P(),
        ),
        out_specs=P("batch", None, "grp"),
        check_vma=False,
    )
```

```python
import jax
import jax.numpy as jnp
from jax import lax
from jax.experimental import pallas as pl
from jax.experimental.pallas import tpu as pltpu
from jax.sharding import PartitionSpec as P

MESH = pl.DeviceIdType.MESH
DEPTH = 4
SPLIT = 4
PARTS = 1
ITEMS = 14


def one_hot(rows, cols, target):
    row = lax.broadcasted_iota(jnp.int32, (rows, cols), 0)
    col = lax.broadcasted_iota(jnp.int32, (rows, cols), 1)
    return (col == target(row)).astype(jnp.float32).astype(jnp.bfloat16)


def sigmoid(x):
    return 0.5 * jnp.tanh(0.5 * x) + 0.5


def matmul(a, b):
    return jnp.dot(a, b, preferred_element_type=jnp.float32)


def kernel(
    tokens_hbm, win_ref, wrec_ref, bias_hbm, table_hbm, out_ref,
    tokens_ref, bias_ref, table_ref, w, wperm, x, proj, s0, s1, obuf, r, cell, pt,
    local_sem, wsend, wrecv, xsend, xrecv, ssend, srecv, osend, orecv, gsend, grecv, done,
):
    groups = lax.axis_size("grp") // SPLIT
    ring = lax.axis_size("batch")
    q = lax.axis_index("grp")
    z = lax.axis_index("batch")
    g = q // SPLIT
    m = q % SPLIT
    mates = (m + 1 - 2 * (m % 2), (m + 2) % SPLIT, SPLIT - 1 - m)

    here = m // 2 * 2

    def mate(d):
        return (g * SPLIT + mates[d], z)

    up = (q, (z + 1) % ring)
    down = (q, (z + ring - 1) % ring)

    loads = []
    for layer in range(2):
        for kind, ref in enumerate((win_ref, wrec_ref)):
            arr = 2 * layer + kind
            load = pltpu.make_async_copy(
                ref.at[layer], w.at[arr, pl.ds(z * 8, 8)], local_sem.at[arr]
            )
            load.start()
            loads.append(load)

    small = []
    for n, (ref, copy) in enumerate(
        ((tokens_hbm, tokens_ref), (bias_hbm, bias_ref), (table_hbm, table_ref))
    ):
        load = pltpu.make_async_copy(ref, copy, local_sem.at[4 + n])
        load.start()
        small.append(load)

    barrier = pltpu.get_barrier_semaphore()
    for device in (up, down, mate(0), mate(1), mate(2)):
        pl.semaphore_signal(barrier, inc=1, device_id=device, device_id_type=MESH)

    @pl.loop(1, groups)
    def _(d):
        other = (g + d) % groups
        pl.semaphore_signal(
            barrier, inc=1, device_id=(other * SPLIT + m, z), device_id_type=MESH
        )

    def item(n, way, came):
        arr, j = n // ITEMS, n % ITEMS
        hop, piece = j // DEPTH, j % DEPTH
        if way == 0:
            origin = (z + 2 * ring - hop - came) % ring
            device = up
        else:
            piece = (piece + DEPTH // 2) % DEPTH
            origin = (z + hop + came) % ring
            device = down
        view = w.at[arr, pl.ds(origin * 8 + piece * 2, 2)]
        return pltpu.make_async_remote_copy(
            src_ref=view, dst_ref=view, send_sem=wsend.at[n, way], recv_sem=wrecv.at[n, way],
            device_id=device, device_id_type=MESH,
        )

    def tick(n, more=True):
        for way in range(2):
            item(n, way, 1).wait_recv()
            if more:
                item(n + DEPTH, way, 0).start()
            item(n, way, 0).wait_send()

    def state_copy(states, layer, t, h, d, owner):
        view = states.at[t, h, owner]
        return pltpu.make_async_remote_copy(
            src_ref=view, dst_ref=view,
            send_sem=ssend.at[layer, t, h, d], recv_sem=srecv.at[layer, t, h, d],
            device_id=mate(d), device_id_type=MESH,
        )

    def input_copy(d, owner):
        view = x.at[owner]
        return pltpu.make_async_remote_copy(
            src_ref=view, dst_ref=view, send_sem=xsend.at[d], recv_sem=xrecv.at[d],
            device_id=mate(d), device_id_type=MESH,
        )

    def mixed_copy(p, d, owner):
        view = r.at[p, owner]
        return pltpu.make_async_remote_copy(
            src_ref=view, dst_ref=view, send_sem=gsend.at[p, d], recv_sem=grecv.at[p, d],
            device_id=mate(d), device_id_type=MESH,
        )

    def shuffled_all(p):
        return pltpu.make_async_remote_copy(
            src_ref=obuf.at[p, pl.ds(0, groups - 1)], dst_ref=r.at[p, m, pl.ds(0, groups - 1)],
            send_sem=osend.at[p], recv_sem=orecv.at[p], device_id=mate(0), device_id_type=MESH,
        )

    loads[0].wait()
    pl.semaphore_wait(barrier, 5 + groups - 1)
    for n in range(DEPTH):
        for way in range(2):
            item(n, way, 0).start()

    for load in small + loads[1:]:
        load.wait()

    rows = tokens_ref.shape[0]
    steps = proj.shape[0]
    seqs = rows // steps
    part = seqs // PARTS
    order = one_hot(rows, rows, lambda a: (a & (seqs - 1)) * steps + (a >> seqs.bit_length() - 1))
    x[m] = matmul(order, tokens_ref[...]).astype(jnp.bfloat16)
    for d in (2, 1, 0):
        input_copy(d, m).start()
    for n in range(2):
        tick(n)

    lanes = 128
    per_row = lanes // 4
    odd = q // per_row
    row = lax.broadcasted_iota(jnp.int32, (lanes, lanes), 0)
    col = lax.broadcasted_iota(jnp.int32, (lanes, lanes), 1)
    mine = ((col >> 2) == q % per_row) & ((row & 1) == odd)
    entries = jnp.where(mine, table_ref[...] - q * 256, 0).astype(jnp.float32).astype(jnp.bfloat16)
    spread = matmul(one_hot(256, lanes, lambda a: (a >> 2) * 2 + odd), entries)
    row = lax.broadcasted_iota(jnp.int32, (256, lanes), 0)
    col = lax.broadcasted_iota(jnp.int32, (256, lanes), 1)
    wanted = col == (q % per_row) * 4 + (row & 3)
    picked = jnp.sum(jnp.where(wanted, spread, 0.0), axis=1, keepdims=True)
    channel = lax.broadcasted_iota(jnp.int32, (256, 256), 1).astype(jnp.float32)
    pt[...] = jnp.where(channel == picked, 1.0, 0.0).astype(jnp.bfloat16)

    def rows_of(arr, i):
        return w.at[arr, pl.ds(i * 16, 16)]

    @pl.loop(2, ITEMS)
    def _(n):
        tick(n)

    for d in range(3):
        input_copy(d, mates[d]).wait_recv()
        input_copy(d, m).wait_send()

    @pl.loop(0, 4)
    def _(c):
        cols = pl.ds(pl.multiple_of(c * 256, 256), 256)
        total = bias_ref[0:1, cols]
        for i in range(SPLIT):
            total = total + matmul(x[i], w[0, pl.ds(i * 16, 16), :, cols].reshape(256, 256))
        proj[:, :, :, cols] = total.reshape(steps, PARTS, part, 256)
        tick(ITEMS + c)

    def update(gate, states, layer, t, h, first=False):
        ingate = sigmoid(gate(0))
        cellgate = jnp.tanh(gate(2))
        now = ingate * cellgate
        if not first:
            now = now + sigmoid(gate(1)) * cell[h]
        outgate = sigmoid(gate(3))
        cell[h] = now
        states[t, h, m] = (outgate * jnp.tanh(now)).astype(jnp.bfloat16)

    def send_state(states, layer, t, h):
        for d in (1, 2, 0):
            state_copy(states, layer, t, h, d, m).start()

    def start(states, layer):
        for h in range(PARTS):
            update(lambda k: proj[0, h, :, k * 256 : k * 256 + 256], states, layer, 0, h, first=True)
            send_state(states, layer, 0, h)

    def step(states, layer, t, h, between=None):
        arr = 2 * layer + 1

        state_copy(states, layer, t - 1, h, 0, mates[0]).wait_recv()
        near = jnp.concatenate([states[t - 1, h, here + i] for i in range(2)], axis=1)
        pre = proj[t, h] + matmul(near, w[arr, pl.ds(here * 16, 32)].reshape(512, 1024))
        if between is not None:
            between()
        for d in (1, 2):
            state_copy(states, layer, t - 1, h, d, mates[d]).wait_recv()
            far = states[t - 1, h, mates[d]]
            pre = pre + matmul(far, w[arr, pl.ds(mates[d] * 16, 16)].reshape(256, 1024))
        update(lambda k: pre[:, k * 256 : k * 256 + 256], states, layer, t, h)

        @pl.when(t < steps - 1)
        def _():
            send_state(states, layer, t, h)

        for d in range(3):
            state_copy(states, layer, t - 1, h, d, m).wait_send()

    def forward(p):
        shuffled_all(p).wait_recv()
        for d in range(3):
            mixed_copy(p, d, m).start()

    start(s0, 0)

    @pl.loop(ITEMS + 4, 2 * ITEMS)
    def _(n):
        tick(n)

    @pl.loop(1, steps)
    def _(t):
        p = t // 2
        n = 2 * ITEMS + 3 * (t - 1)
        step(s0, 0, t, 0, between=lambda: tick(n))
        for h in range(1, PARTS):
            step(s0, 0, t, h)
        tick(n + 1)

        @pl.when(t % 2 == 1)
        def _():
            pair = jnp.concatenate([s0[t - 1 + h // PARTS, h % PARTS, m] for h in range(2 * PARTS)], axis=0)
            moved = lax.dot_general(
                pt[...], pair, (((1,), (1,)), ((), ())), preferred_element_type=jnp.float32
            )
            obuf[p] = moved.astype(jnp.bfloat16).reshape(groups, 16, 128)
            r[p, m, g] = obuf[p, g]

            @pl.loop(1, groups)
            def _(d):
                other = (g + d) % groups
                pltpu.make_async_remote_copy(
                    src_ref=obuf.at[p, other], dst_ref=r.at[p, m, g],
                    send_sem=osend.at[p], recv_sem=orecv.at[p],
                    device_id=(other * SPLIT + m, z), device_id_type=MESH,
                ).start()

        @pl.when(t % 2 == 0)
        def _():
            forward(p - 1)

        tick(n + 2)

    swap = one_hot(
        256, 256, lambda a: (a & 192) + ((a >> 2) & 3) * 16 + ((a >> 4) & 3) * 4 + (a & 3)
    )

    @pl.loop(0, groups // 4)
    def _(v):
        block = jnp.concatenate(
            [w[2, j * 16 + 4 * v + i] for i in range(4) for j in range(SPLIT)], axis=0
        )
        block = matmul(swap, block).astype(jnp.bfloat16).reshape(4, SPLIT, 16, 1024)
        for i in range(4):
            for j in range(SPLIT):
                wperm[j * 16 + 4 * v + i] = block[i, j]

        @pl.when(v % 2 == 1)
        def _():
            tick(4 * ITEMS - 7 + v // 2)

    tick(4 * ITEMS - 5)

    def project_mixed(p):
        shuffled_all(p).wait_send()
        for d in range(3):
            mixed_copy(p, d, mates[d]).wait_recv()
            mixed_copy(p, d, m).wait_send()
        total = lax.dot_general(
            r[p].reshape(1024, 128), wperm[...].reshape(1024, 1024),
            (((0,), (0,)), ((), ())), preferred_element_type=jnp.float32,
        )
        proj[pl.ds(2 * p, 2)] = (total + bias_ref[1:2, :]).reshape(2, PARTS, part, 1024)

    project_mixed(0)

    def stored(t):
        return pltpu.make_async_copy(s1.at[t, 0, m], out_ref.at[t], done.at[t])

    def store(t):
        stored(t).start()

    start(s1, 1)
    forward(steps // 2 - 1)

    @pl.loop(1, steps // 2 - 1)
    def _(p):
        project_mixed(p)

    for n in range(4 * ITEMS - DEPTH, 4 * ITEMS - 1):
        tick(n, False)
    project_mixed(steps // 2 - 1)
    tick(4 * ITEMS - 1, False)

    @pl.loop(1, steps)
    def _(t):
        for h in range(PARTS):
            step(s1, 1, t, h)
        store(t - 1)

    store(steps - 1)

    @pl.loop(0, steps)
    def _(t):
        stored(t).wait()


def local(tokens, input_weights, recur_weights, biases, shuffle):
    seqs, steps, units = tokens.shape
    depth = input_weights.shape[1]
    bf16 = jnp.bfloat16
    hbm = pl.BlockSpec(memory_space=pl.ANY)
    dma = pltpu.SemaphoreType.DMA
    pairs = steps // 2
    out = pl.pallas_call(
        kernel,
        out_shape=jax.ShapeDtypeStruct((steps, seqs, units), bf16),
        in_specs=[hbm] * 5,
        out_specs=hbm,
        scratch_shapes=[
            pltpu.VMEM((seqs * steps, units), bf16),
            pltpu.VMEM((2, 1024), jnp.float32),
            pltpu.VMEM((128, 128), jnp.int32),
            pltpu.VMEM((4, 64, 16, 1024), bf16),
            pltpu.VMEM((64, 16, 1024), bf16),
            pltpu.VMEM((SPLIT, seqs * steps, units), bf16),
            pltpu.VMEM((steps, PARTS, seqs // PARTS, 1024), jnp.float32),
            pltpu.VMEM((steps, PARTS, SPLIT, seqs // PARTS, units), bf16),
            pltpu.VMEM((steps, PARTS, SPLIT, seqs // PARTS, units), bf16),
            pltpu.VMEM((pairs, 16, 16, 128), bf16),
            pltpu.VMEM((pairs, SPLIT, 16, 16, 128), bf16),
            pltpu.VMEM((PARTS, seqs // PARTS, units), jnp.float32),
            pltpu.VMEM((256, 256), bf16),
            dma((7,)),
            dma((4 * ITEMS, 2)),
            dma((4 * ITEMS, 2)),
            dma((3,)),
            dma((3,)),
            dma((2, steps, PARTS, 3)),
            dma((2, steps, PARTS, 3)),
            dma((pairs,)),
            dma((pairs,)),
            dma((pairs, 3)),
            dma((pairs, 3)),
            dma((steps,)),
        ],
        compiler_params=pltpu.CompilerParams(
            collective_id=0, has_side_effects=True, vmem_limit_bytes=63 * 1024 * 1024
        ),
    )(
        tokens.reshape(seqs * steps, units),
        input_weights.reshape(2, depth // 16, 16, 1024),
        recur_weights.reshape(2, depth // 16, 16, 1024),
        biases,
        shuffle.reshape(128, 128),
    )
    return jnp.transpose(out, (1, 0, 2))


def solution(mesh):
    return jax.shard_map(
        local,
        mesh=mesh,
        in_specs=(
            P("batch", None, "grp"),
            P(None, "batch", "grp"),
            P(None, "batch", "grp"),
            P(None, "grp"),
            P(),
        ),
        out_specs=P("batch", None, "grp"),
        check_vma=False,
    )
```
